32 devices in a mesh: section: 4 (over y, x), row: 8 (over z, core).
Axes of the slice: x: 2, y: 2, z: 4, core: 2. Of those that a mesh axis runs over, the one named last changes fastest.
Arguments:
- features: bfloat16 [4, 4, 32, 256, 128], P('section', None, 'row'), may hold values from -6 to 6
- conv_weight: bfloat16 [4, 1152, 128], P('section'), may hold values from -0.1875 to 0.1875
- norm_gain: float32 [4, 128], P('section'), may hold values from 0.5 to 1.5
- norm_bias: float32 [4, 128], P('section'), may hold values from -3 to 3
- valid_mask: int32 [4, 4, 32, 256], P(None, None, 'row'), may hold values from 0 to 1
- out_cotangent: bfloat16 [4, 4, 32, 256, 128], P('section', None, 'row'), may hold values from -6 to 6
Outputs:
- neck_output: bfloat16 [4, 4, 32, 256, 128], P('section', None, 'row')
- feature_grad: bfloat16 [4, 4, 32, 256, 128], P('section', None, 'row')
- weight_grad: float32 [4, 1152, 128], P('section', 'row')
- gain_grad: float32 [4, 128], P('section')
- bias_grad: float32 [4, 128], P('section')
The draws below stay inside these ranges and needn't reach their ends.
All inputs are finite; a program needn't handle non-finite values.
Results may differ from the reference program's by a relative error of at most 0.011.
Values may be sent and summed in bfloat16 or wider, within the bound.
No kernel may reach another device: no remote copies, remote signals or barrier semaphores. Data moves between devices by JAX's collectives and lax.ppermute only.
A program may use at most 128 MiB of HBM per device.

```python
import jax
import jax.numpy as jnp
from jax import lax

C = 128
SCENES = 4
COLS = 256
SECTIONS = 4
MICRO = 4
ROWS = 32


def draw_valid_mask(key, part):
    key = jax.random.fold_in(key, 7)
    mask_shape = (MICRO, SCENES, ROWS, COLS)
    row_index = lax.broadcasted_iota(jnp.int32, mask_shape, 2)
    threshold = 20 + 60 * row_index // max(ROWS - 1, 1)
    random_draws = jax.random.randint(key, mask_shape, 0, 100)
    return (random_draws < threshold).astype(jnp.int32)


def block_levels(stream_key, dims, pieces, low, largest):
    def one(position, parts):
        heights = jax.random.uniform(jax.random.fold_in(jax.random.fold_in(stream_key, 6), position), (parts,), jnp.float32, low / len(pieces), largest / len(pieces))
        return jnp.repeat(jnp.exp(heights), dims[position] // parts).reshape((-1,) + (1,) * (len(dims) - position - 1))

    level = one(*pieces[0])
    for cut in pieces[1:]:
        level = level * one(*cut)
    return level


def noise(rng, extent, width, limit, shards=(), dtype=jnp.bfloat16):
    gain = block_levels(rng, extent, shards, -0.22, 0.18) if shards else 1.0
    values = jax.random.normal(rng, extent, jnp.float32) * width * gain
    return jnp.minimum(jnp.maximum(values, -limit), limit).astype(dtype)


def setup_inputs(seed: int = 0) -> dict:
    arg_keys = jax.random.split(jax.random.key(seed), 7)
    return {
        "features": noise(arg_keys[0], (MICRO, SCENES, ROWS, COLS, C), 1.0, 6.0, ((0, 4), (2, 8))),
        "conv_weight": noise(arg_keys[1], (SECTIONS, 9 * C, C), (9 * C) ** -0.5, 0.1875, ((0, 4),)),
        "norm_gain": jnp.clip(1.0 + 0.1 * jax.random.normal(arg_keys[2], (SECTIONS, C), jnp.float32), 0.5, 1.5),
        "norm_bias": noise(arg_keys[3], (SECTIONS, C), 0.5, 3.0, ((0, 4),), jnp.float32),
        "valid_mask": draw_valid_mask(jax.random.fold_in(arg_keys[6], 71), 0),
        "out_cotangent": noise(arg_keys[5], (MICRO, SCENES, ROWS, COLS, C), 1.0, 6.0, ((0, 4), (2, 8))),
    }


norm_eps = 1e-05

@jax.custom_vjp
def low(v):
    return lax.optimization_barrier(v.astype(jnp.bfloat16)).astype(jnp.float32)

@jax.custom_vjp
def low_back(v):
    return v

def low_keep(v):
    return (low(v), None)

def low_pass(kept, grad):
    return (grad,)

def back_keep(v):
    return (v, None)

def back_low(kept, grad):
    return (low(grad),)
low.defvjp(low_keep, low_pass)
low_back.defvjp(back_keep, back_low)

def convolve(field, kernel_flat):
    kernel = kernel_flat.reshape(3, 3, C, C)
    return lax.conv_general_dilated(field, kernel, (1, 1), ((1, 1), (1, 1)), dimension_numbers=('NHWC', 'HWIO', 'NHWC'), precision=lax.Precision.HIGHEST)

def forward(inputs, weights, gains, biases, voxel_mask):
    current = inputs
    for section_num in range(SECTIONS):
        weight_mask = voxel_mask if section_num == 0 else jnp.ones_like(voxel_mask)
        masked = current * weight_mask
        pre_norm = low_back(convolve(masked, weights[section_num]))
        voxel_count = jnp.sum(weight_mask)
        row_mean = lax.optimization_barrier(jnp.sum(weight_mask * pre_norm, axis=(0, 1, 2))) / voxel_count
        variance = lax.optimization_barrier(jnp.sum(weight_mask * pre_norm * pre_norm, axis=(0, 1, 2))) / voxel_count - row_mean * row_mean
        normed = (pre_norm - row_mean) * lax.rsqrt(variance + norm_eps)
        activ = jax.nn.silu(normed * gains[section_num] + biases[section_num])
        current = low_back(low(masked + weight_mask * activ))
    return current

def reference(features, conv_weight, norm_gain, norm_bias, valid_mask, out_cotangent):
    weights = conv_weight.astype(jnp.float32)
    gains = norm_gain.astype(jnp.float32)
    biases = norm_bias.astype(jnp.float32)

    def one_micro(running, micro_items):
        inputs, mask_ints, cotangent = micro_items
        voxel_mask = mask_ints.astype(jnp.float32)[..., None]

        def forward_here(input_arr, weight_arr, gain_arr, bias_arr):
            return forward(input_arr, weight_arr, gain_arr, bias_arr, voxel_mask)
        result, pullback = jax.vjp(forward_here, inputs.astype(jnp.float32), weights, gains, biases)
        grad_input, grad_weight, grad_gain, grad_bias = pullback(cotangent.astype(jnp.float32))
        running = (running[0] + grad_weight, running[1] + grad_gain, running[2] + grad_bias)
        return (running, (result.astype(jnp.bfloat16), grad_input.astype(jnp.bfloat16)))
    start = (jnp.zeros(weights.shape, jnp.float32), jnp.zeros(gains.shape, jnp.float32), jnp.zeros(biases.shape, jnp.float32))
    sums_all, stacked = lax.scan(one_micro, start, (features, valid_mask, out_cotangent))
    return (stacked[0], stacked[1], sums_all[0], sums_all[1], sums_all[2])
```

```python
import functools

import jax
import jax.numpy as jnp
from jax import lax
from jax.experimental import pallas as pl
from jax.experimental.pallas import tpu as pltpu
from jax.sharding import PartitionSpec as P

norm_eps = 1e-05
hole = -1e30
hole_edge = -1e29
f32 = jnp.float32
bf16 = jnp.bfloat16
VMEM_SPEC = pl.BlockSpec(memory_space=pltpu.VMEM)
SMEM_SPEC = pl.BlockSpec(memory_space=pltpu.SMEM)


def shifted(value, step):
    cols = value.shape[0]
    index = lax.broadcasted_iota(jnp.int32, value.shape, 0)
    edge = 0 if step == 1 else cols - 1
    return jnp.where(index == edge, 0.0, pltpu.roll(value, step % cols, 0))


def put_row(stack, scene, k, value, flip):
    ch = value.shape[1]
    lanes = slice((k % 2) * ch, (k % 2 + 1) * ch)
    before, after = (2, 0) if flip else (0, 2)
    stack[1, k // 2, scene, :, lanes] = value.astype(bf16)
    stack[before, k // 2, scene, :, lanes] = shifted(value, 1).astype(bf16)
    stack[after, k // 2, scene, :, lanes] = shifted(value, -1).astype(bf16)


def put_blocks(kernel_rows, blocks):
    ch = kernel_rows.shape[1]

    def tap(i, j):
        return kernel_rows[(3 * i + j) * ch : (3 * i + j + 1) * ch, :]

    zero = jnp.zeros((ch, ch), bf16)
    for j in range(3):
        blocks[2 * j, :ch, :ch] = tap(0, j)
        blocks[2 * j, :ch, ch:] = zero
        blocks[2 * j, ch:, :ch] = tap(1, j)
        blocks[2 * j, ch:, ch:] = tap(0, j)
        blocks[2 * j + 1, :ch, :ch] = tap(2, j)
        blocks[2 * j + 1, :ch, ch:] = tap(1, j)
        blocks[2 * j + 1, ch:, :ch] = zero
        blocks[2 * j + 1, ch:, ch:] = tap(2, j)


def conv_pair(stack, blocks, scene, p):
    lhs = jnp.concatenate([stack[j, p + h, scene] for j in range(3) for h in range(2)], axis=1)
    rhs = jnp.concatenate([blocks[n] for n in range(6)], axis=0)
    return jnp.dot(lhs, rhs, preferred_element_type=f32)


def conv_back_pair(stack, blocks, scene, p):
    total = None
    for j in range(3):
        for h in range(2):
            term = lax.dot_general(
                stack[j, p + h, scene],
                blocks[2 * j + 1 - h],
                (((1,), (1,)), ((), ())),
                preferred_element_type=f32,
            )
            total = term if total is None else total + term
    return total


def summed(pieces):
    total = pieces[0][...]
    for piece in pieces[1:]:
        total = total + piece[...]
    return total


def norm_stats(total, count):
    count = total[2:3] if count is None else count
    mean = total[0:1] / count
    inv = lax.rsqrt(total[1:2] / count - mean * mean + norm_eps)
    return mean, inv, count


def half_affine(mean, inv, gb):
    scale = inv * gb[0:1]
    return 0.5 * scale, 0.5 * (gb[1:2] - mean * scale)


def slope_of(pre, scale, offset):
    half = pre * scale + offset
    t = jnp.tanh(half)
    return (0.5 + 0.5 * t) * (1.0 + half * (1.0 - t))


def fold(value):
    return jnp.sum(value.reshape(-1, 8, value.shape[-1]), axis=0)


def put_sums(ref, first, second, third=None):
    ch = ref.shape[1]
    ref[0:1, :] = jnp.sum(first, axis=0, keepdims=True)
    ref[1:2, :] = jnp.sum(second, axis=0, keepdims=True)
    ref[2:3, :] = jnp.zeros((1, ch), f32) if third is None else third
    ref[3:8, :] = jnp.zeros((5, ch), f32)


def mask_columns(rows):
    count, cols = rows.shape
    filled = jnp.concatenate([rows, jnp.zeros((128 - count, cols), f32)], axis=0)
    return filled.T


def prep_kernel(sc, mask, features, cot, weight, gb, e1, e2, wsend):
    scenes, rows, cols, ch = features.shape
    even = sc[0] == 0
    near = jnp.where(even, rows - 1, 0)
    columns = mask_columns(mask[...])
    for scene in range(scenes):
        low = features[scene, 0].astype(f32) * columns[:, scene * rows : scene * rows + 1]
        last = scene * rows + rows - 1
        high = features[scene, rows - 1].astype(f32) * columns[:, last : last + 1]
        e1[0, scene] = jnp.where(even, high, low).astype(bf16)
        e2[0, scene] = jnp.where(even, low, high).astype(bf16)
        e1[1, scene] = cot[scene, near]
        e2[1, scene] = cot[scene, rows - 1 - near]
    half = weight.shape[0] // 2
    wsend[:half] = weight[pl.ds(pl.multiple_of(sc[0] * half, 16), half), :]
    hi = gb[...].astype(bf16)
    left = gb[...] - hi.astype(f32)
    mid = left.astype(bf16)
    low = (left - mid.astype(f32)).astype(bf16)
    wsend[half:] = jnp.concatenate([hi.astype(f32), mid.astype(f32), low.astype(f32), jnp.zeros_like(left)], axis=0).astype(bf16)


def gather_kernel(sc, own, gb, r1, r2, r3, other, weights, gbs):
    half = own.shape[0] // 2
    here = sc[1]
    mine = pl.ds(pl.multiple_of(sc[0] * half, 16), half)
    theirs = pl.ds(pl.multiple_of((1 - sc[0]) * half, 16), half)
    weights[here] = own[...]
    gbs[here] = gb[...]
    for d, got in ((1, r1), (2, r2), (3, r3)):
        there = sc[1 + d]
        weights[there, mine, :] = got[:half]
        weights[there, theirs, :] = other[d - 1, :half]
        parts = got[half:].astype(f32)
        gbs[there] = parts[0:8] + parts[8:16] + parts[16:24]


def edges_of(sc, e1, e2):
    even = sc[0] == 0
    return jnp.where(even, e2, e1), jnp.where(even, e1, e2)


def finish_forward(sc, stack, blocks, pre, e1s, e2s, sums, scenes, rows, make_rows, columns):
    first = second = None
    make_rows(0)
    for scene in range(scenes):
        if scene + 1 < scenes:
            make_rows(scene + 1)
        for p in range(rows // 2):
            both = conv_pair(stack, blocks, scene, p)
            ch = both.shape[1] // 2
            for n in range(2):
                row = both[:, n * ch : (n + 1) * ch]
                kept = row
                if columns is not None:
                    at = scene * rows + 2 * p + n
                    inside = columns[:, at : at + 1] > 0.5
                    kept = jnp.where(inside, row, hole)
                    row = jnp.where(inside, row, 0.0)
                pre[scene, 2 * p + n] = kept
                one, two = fold(row), fold(row * row)
                first = one if first is None else first + one
                second = two if second is None else second + two
        near = jnp.where(sc[0] == 0, rows - 1, 0)
        e1s[scene] = pre[scene, near].astype(bf16)
        e2s[scene] = pre[scene, rows - 1 - near].astype(bf16)
    return first, second


def first_kernel(sc, mask, features, e1, e2, weights, xp, pre, e1s, e2s, sums, stack, blocks):
    scenes, rows, cols, ch = features.shape
    put_blocks(weights.at[0], blocks)
    columns = mask_columns(mask[...])

    def make_rows(scene):
        top, bottom = edges_of(sc, e1[0, scene], e2[0, scene])
        for k in range(rows + 2):
            if k == 0:
                value = top.astype(f32)
            elif k == rows + 1:
                value = bottom.astype(f32)
            else:
                at = scene * rows + k - 1
                value = features[scene, k - 1].astype(f32) * columns[:, at : at + 1]
            xp[scene, k] = value.astype(bf16)
            put_row(stack, scene, k, value, False)

    first, second = finish_forward(sc, stack, blocks, pre, e1s, e2s, sums, scenes, rows, make_rows, columns)
    total = jnp.sum(jnp.sum(mask[...], axis=1, keepdims=True), axis=0, keepdims=True)
    put_sums(sums, first, second, jnp.broadcast_to(total, (1, ch)))


def next_kernel(section, count, n, sc, xp_in, pre_in, e1, e2, *rest):
    pieces, rest = rest[:n], rest[n:]
    gbs, weights, xp, pre, e1s, e2s, sums, stack, blocks = rest
    scenes, rows, cols, ch = pre_in.shape
    put_blocks(weights.at[section], blocks)
    mean, inv, _ = norm_stats(summed(pieces), count)
    scale, offset = half_affine(mean, inv, gbs[section - 1])
    inside_top = sc[5].astype(f32)
    inside_bottom = sc[6].astype(f32)

    def make_rows(scene):
        top, bottom = edges_of(sc, e1[scene], e2[scene])
        for k in range(rows + 2):
            if k == 0:
                value = top.astype(f32)
            elif k == rows + 1:
                value = bottom.astype(f32)
            else:
                value = pre_in[scene, k - 1]
            half = value * scale + offset
            act = half * jnp.tanh(half) + half
            if count is None:
                act = jnp.where(value > hole_edge, act, 0.0)
            if k == 0:
                act = act * inside_top
            elif k == rows + 1:
                act = act * inside_bottom
            value = xp_in[scene, k].astype(f32) + act
            xp[scene, k] = value.astype(bf16)
            put_row(stack, scene, k, value, False)

    first, second = finish_forward(sc, stack, blocks, pre, e1s, e2s, sums, scenes, rows, make_rows, None)
    put_sums(sums, first, second)


def turn_kernel(count, n, section, xp, pre, cot, *rest):
    pieces, rest = rest[:n], rest[n:]
    gbs, neck, grad_u, sums = rest
    scenes, rows, cols, ch = pre.shape
    mean, inv, _ = norm_stats(summed(pieces), count)
    scale, offset = half_affine(mean, inv, gbs[section])
    first = second = None
    for scene in range(scenes):
        for r in range(rows):
            value = pre[scene, r]
            half = value * scale + offset
            t = jnp.tanh(half)
            act = half * t + half
            neck[scene, r] = (xp[scene, r + 1].astype(f32) + act).astype(bf16)
            grad = cot[scene, r].astype(f32) * ((0.5 + 0.5 * t) * (1.0 + half * (1.0 - t)))
            grad_u[scene, r] = grad
            one, two = fold(grad * ((value - mean) * inv)), fold(grad)
            first = one if first is None else first + one
            second = two if second is None else second + two
    put_sums(sums, first, second)


def back_kernel(section, count, count_below, n, sc, *rest):
    pieces, rest = rest[:n], rest[n:]
    grads, rest = rest[:n], rest[n:]
    below = section > 0
    if below:
        pieces_below, rest = rest[:n], rest[n:]
        pre_below, rest = rest[0], rest[1:]
    grad_u, grad_in, g1, g2, pre, p1, p2, gbs, weights, *rest = rest
    if below:
        stack, grad_out, grad_u_below, e1s, e2s, sums, total_out, blocks = rest
    else:
        stack, grad_out, total_out, blocks = rest
    scenes, rows, cols, ch = pre.shape
    masked = count is None
    put_blocks(weights.at[section], blocks)
    mean, inv, cells = norm_stats(summed(pieces), count)
    gb = gbs[section]
    scale, offset = half_affine(mean, inv, gb)
    total = summed(grads)
    total_out[...] = total
    lead = inv * gb[0:1]
    by_pre = -lead * inv * total[0:1] / cells
    constant = -lead * total[1:2] / cells - by_pre * mean
    inside_top = sc[5].astype(f32)
    inside_bottom = sc[6].astype(f32)
    if below:
        mean_below, inv_below, _ = norm_stats(summed(pieces_below), count_below)
        scale_below, offset_below = half_affine(mean_below, inv_below, gbs[section - 1])

    def make_rows(scene):
        g_top, g_bottom = edges_of(sc, g1[scene], g2[scene])
        p_top, p_bottom = edges_of(sc, p1[scene], p2[scene])
        for k in range(rows + 2):
            if 0 < k < rows + 1:
                value = pre[scene, k - 1]
                lifted = grad_u[scene, k - 1]
            else:
                value = (p_top if k == 0 else p_bottom).astype(f32)
                lifted = (g_top if k == 0 else g_bottom).astype(f32) * slope_of(value, scale, offset)
            out = lead * lifted + (by_pre * value + constant)
            if masked:
                out = jnp.where(value > hole_edge, out, 0.0)
            if k == 0:
                out = out * inside_top
            elif k == rows + 1:
                out = out * inside_bottom
            put_row(stack, scene, k, out, True)

    first = second = None
    make_rows(0)
    for scene in range(scenes):
        if scene + 1 < scenes:
            make_rows(scene + 1)
        for p in range(rows // 2):
            both = conv_back_pair(stack, blocks, scene, p)
            for m in range(2):
                r = 2 * p + m
                grad = grad_in[scene, r].astype(f32) + both[:, m * ch : (m + 1) * ch]
                if masked:
                    grad = jnp.where(pre[scene, r] > hole_edge, grad, 0.0)
                grad = grad.astype(bf16)
                grad_out[scene, r] = grad
                if below:
                    value = pre_below[scene, r]
                    lifted = grad.astype(f32) * slope_of(value, scale_below, offset_below)
                    if count_below is None:
                        lifted = jnp.where(value > hole_edge, lifted, 0.0)
                        value = jnp.where(value > hole_edge, value, 0.0)
                    grad_u_below[scene, r] = lifted
                    one, two = fold(lifted * ((value - mean_below) * inv_below)), fold(lifted)
                    first = one if first is None else first + one
                    second = two if second is None else second + two
        if below:
            near = jnp.where(sc[0] == 0, rows - 1, 0)
            e1s[scene] = grad_out[scene, near]
            e2s[scene] = grad_out[scene, rows - 1 - near]
    if below:
        put_sums(sums, first, second)


def weight_kernel(xp, stack, out):
    scenes, padded, cols, ch = xp.shape
    rows = padded - 2
    total = None
    for scene in range(scenes):
        lhs = jnp.concatenate(
            [xp[scene, i : i + rows].reshape(rows * cols, ch) for i in range(3)], axis=1
        )
        rhs = jnp.concatenate(
            [
                jnp.concatenate(
                    [
                        stack[j, k // 2, scene, :, (k % 2) * ch : (k % 2 + 1) * ch]
                        for j in range(3)
                    ],
                    axis=1,
                )
                for k in range(1, rows + 1)
            ],
            axis=0,
        )
        term = lax.dot_general(lhs, rhs, (((0,), (0,)), ((), ())), preferred_element_type=f32)
        total = term if total is None else total + term
    for i in range(3):
        for j in range(3):
            out[(3 * i + j) * ch : (3 * i + j + 1) * ch, :] = total[
                i * ch : (i + 1) * ch, j * ch : (j + 1) * ch
            ]


def call(body, outs, ins, scratch=(), smem=0, flops=0, name=None):
    return pl.pallas_call(
        body,
        out_shape=[jax.ShapeDtypeStruct(s, d) for s, d in outs],
        in_specs=[SMEM_SPEC] * smem + [VMEM_SPEC] * (len(ins) - smem),
        out_specs=[VMEM_SPEC] * len(outs),
        scratch_shapes=list(scratch),
        compiler_params=pltpu.CompilerParams(vmem_limit_bytes=40 * 2**20),
        cost_estimate=pl.CostEstimate(flops=flops, bytes_accessed=0, transcendentals=0),
        name=name,
    )(*ins)


def swap(value, axis, step):
    count = lax.axis_size(axis)
    return lax.ppermute(value, axis, [(i, i ^ step) for i in range(count)])


def swap_next(value, axis):
    count = lax.axis_size(axis)
    pairs = []
    for i in range(1, count - 1, 2):
        pairs += [(i, i + 1), (i + 1, i)]
    return lax.ppermute(value, axis, pairs)


def row_pieces(value):
    count = lax.axis_size("row")
    total = value + swap(value, "row", 1)
    stride = 2
    while True:
        group = min(4, count // stride)
        pieces = [total] + [swap(total, "row", k * stride) for k in range(1, group)]
        stride *= group
        if stride >= count:
            return pieces
        total = sum(pieces[1:], pieces[0])


def per_device(features, conv_weight, norm_gain, norm_bias, valid_mask, out_cotangent):
    sections = lax.axis_size("section")
    tiles = lax.axis_size("row")
    here = lax.axis_index("section")
    tile = lax.axis_index("row")
    scenes, rows, cols, ch = features.shape[1:]
    taps = conv_weight.shape[1]
    cells = float(scenes * rows * cols * tiles)
    x = features[0]
    cot = out_cotangent[0]
    own = conv_weight[0]
    gb = jnp.concatenate([norm_gain, norm_bias, jnp.zeros((6, ch), f32)], axis=0)
    mask = lax.dynamic_index_in_dim(valid_mask, here, 0, keepdims=False)
    mask = mask.reshape(scenes * rows, cols).astype(f32)
    sc = jnp.stack(
        [
            tile % 2,
            here,
            here ^ 1,
            here ^ 2,
            here ^ 3,
            (tile > 0).astype(jnp.int32),
            (tile < tiles - 1).astype(jnp.int32),
        ]
    ).astype(jnp.int32)
    tile_shape = (scenes, rows, cols, ch)
    pad_shape = (scenes, rows + 2, cols, ch)
    edge_shape = (scenes, cols, ch)
    sum_shape = (8, ch)
    stack_shape = (3, rows // 2 + 1, scenes, cols, 2 * ch)
    blocks = pltpu.VMEM((6, 2 * ch, 2 * ch), bf16)
    flops = 2 * scenes * rows * cols * taps * ch
    half = taps // 2

    e1, e2, wsend = call(
        prep_kernel,
        [((2,) + edge_shape, bf16)] * 2 + [((half + 32, ch), bf16)],
        (sc, mask, x, cot, own, gb),
        smem=1,
        name="prep",
    )
    e2 = swap_next(e2, "row")
    e1 = swap(e1, "row", 1)
    got = [swap(wsend, "section", d) for d in (1, 2, 3)]
    other = swap(jnp.stack(got), "row", 1)
    weights, gbs = call(
        gather_kernel,
        [((sections, taps, ch), bf16), ((sections, 8, ch), f32)],
        (sc, own, gb, *got, other),
        smem=1,
        name="gather",
    )
    cot1, cot2 = e1[1], e2[1]

    forward_outs = [
        (pad_shape, bf16),
        (tile_shape, f32),
        (edge_shape, bf16),
        (edge_shape, bf16),
        (sum_shape, f32),
    ]
    scratch = [pltpu.VMEM(stack_shape, bf16), blocks]
    kept = []
    xp, pre, e1s, e2s, sums = call(
        first_kernel,
        forward_outs,
        (sc, mask, x, e1, e2, weights),
        scratch,
        smem=1,
        flops=flops,
        name="forward",
    )
    for section in range(sections):
        count = None if section == 0 else cells
        e2r = swap_next(e2s, "row")
        pieces = row_pieces(sums)
        e1r = swap(e1s, "row", 1)
        kept.append((xp, pre, e1r, e2r, pieces, count))
        if section == sections - 1:
            break
        xp, pre, e1s, e2s, sums = call(
            functools.partial(next_kernel, section + 1, count, len(pieces)),
            forward_outs,
            (sc, xp, pre, e1r, e2r, *pieces, gbs, weights),
            scratch,
            smem=1,
            flops=flops,
            name="forward",
        )
    neck, grad_u, sums = call(
        functools.partial(turn_kernel, cells, len(pieces), sections - 1),
        [(tile_shape, bf16), (tile_shape, f32), (sum_shape, f32)],
        (xp, pre, cot, *pieces, gbs),
        name="turn",
    )
    grad, g1, g2 = cot, cot1, cot2
    parts = [None] * sections
    totals = [None] * sections
    for section in range(sections - 1, -1, -1):
        xp, pre, p1, p2, pieces, count = kept[section]
        grads = row_pieces(sums)
        ins = [sc, *pieces, *grads]
        outs = [(stack_shape, bf16), (tile_shape, bf16)]
        count_below = None
        if section > 0:
            _, pre_below, _, _, pieces_below, count_below = kept[section - 1]
            ins += [*pieces_below, pre_below]
            outs += [(tile_shape, f32), (edge_shape, bf16), (edge_shape, bf16), (sum_shape, f32)]
        outs += [(sum_shape, f32)]
        result = call(
            functools.partial(back_kernel, section, count, count_below, len(pieces)),
            outs,
            (*ins, grad_u, grad, g1, g2, pre, p1, p2, gbs, weights),
            [blocks],
            smem=1,
            flops=flops,
            name="backward",
        )
        stack, grad = result[:2]
        totals[section] = result[-1]
        if section > 0:
            grad_u, e1s, e2s, sums = result[2:6]
            g2 = swap_next(e2s, "row")
            g1 = swap(e1s, "row", 1)
        (part,) = call(
            weight_kernel, [((taps, ch), f32)], (xp, stack), flops=flops, name="weight"
        )
        parts[section] = lax.psum_scatter(part, "row", scatter_dimension=0, tiled=True)
    sending = jnp.stack([jnp.concatenate([p, t], axis=0) for p, t in zip(parts, totals)])
    result = lax.dynamic_index_in_dim(sending, here, 0, keepdims=False)
    for d in (1, 2, 3):
        result = result + swap(
            lax.dynamic_index_in_dim(sending, here ^ d, 0, keepdims=False), "section", d
        )
    chunk = taps // tiles
    return (
        neck[None],
        grad[None],
        result[None, :chunk],
        result[chunk : chunk + 1],
        result[chunk + 1 : chunk + 2],
    )


def solution(mesh):
    return jax.shard_map(
        per_device,
        mesh=mesh,
        in_specs=(
            P("section", None, "row", None, None),
            P("section", None, None),
            P("section", None),
            P("section", None),
            P(None, None, "row", None),
            P("section", None, "row", None, None),
        ),
        out_specs=(
            P("section", None, "row", None, None),
            P("section", None, "row", None, None),
            P("section", "row", None),
            P("section", None),
            P("section", None),
        ),
        check_vma=False,
    )
```

```python
import functools

import jax
import jax.numpy as jnp
from jax import lax
from jax.experimental import pallas as pl
from jax.experimental.pallas import tpu as pltpu
from jax.sharding import PartitionSpec as P

norm_eps = 1e-05
hole = -1e30
hole_edge = -1e29
f32 = jnp.float32
bf16 = jnp.bfloat16
VMEM_SPEC = pl.BlockSpec(memory_space=pltpu.VMEM)


class Place:
    def __init__(self):
        tile = lax.axis_index("row")
        self.section = lax.axis_index("section")
        self.core = lax.rem(tile, 2)
        self.even = self.core == 0
        self.chip = tile // 2
        outer = jnp.where(self.even, 0, lax.axis_size("row") - 1)
        self.inside = (tile != outer).astype(f32)

    def row(self, q, rows):
        return jnp.where(self.even, rows - 1 - q, q)

    def tap(self, i):
        return jnp.where(self.even, 2 - i, i)


def shifted(value, step):
    cols = value.shape[0]
    index = lax.broadcasted_iota(jnp.int32, value.shape, 0)
    edge = 0 if step == 1 else cols - 1
    return jnp.where(index == edge, 0.0, pltpu.roll(value, step % cols, 0))


def shifts(value, flip):
    left, right = shifted(value, 1).astype(bf16), shifted(value, -1).astype(bf16)
    return (right, value.astype(bf16), left) if flip else (left, value.astype(bf16), right)


def put_row(stack, scene, k, value, flip):
    ch = value.shape[1]
    for j, part in enumerate(shifts(value, flip)):
        stack[j, k // 2, scene, :, (k % 2) * ch : (k % 2 + 1) * ch] = part


def put_outer(outer, scene, value, flip):
    for j, part in enumerate(shifts(value, flip)):
        outer[j, scene] = part


def put_blocks(kernel_rows, blocks):
    ch = kernel_rows.shape[1]

    def tap(i, j):
        return kernel_rows[(3 * i + j) * ch : (3 * i + j + 1) * ch, :]

    zero = jnp.zeros((ch, ch), bf16)
    for j in range(3):
        blocks[2 * j, :ch, :ch] = tap(0, j)
        blocks[2 * j, :ch, ch:] = zero
        blocks[2 * j, ch:, :ch] = tap(1, j)
        blocks[2 * j, ch:, ch:] = tap(0, j)
        blocks[2 * j + 1, :ch, :ch] = tap(2, j)
        blocks[2 * j + 1, :ch, ch:] = tap(1, j)
        blocks[2 * j + 1, ch:, :ch] = zero
        blocks[2 * j + 1, ch:, ch:] = tap(2, j)


def operand(stack, outer, scene, j, pair):
    if outer is None or pair + 1 < stack.shape[1]:
        return stack[j, pair, scene]
    ch = outer.shape[-1]
    return jnp.concatenate([stack[j, pair, scene, :, :ch], outer[j, scene]], axis=1)


def conv_pair(stack, outer, blocks, scene, p):
    lhs = [operand(stack, outer, scene, j, p + h) for j in range(3) for h in range(2)]
    rhs = jnp.concatenate([blocks[n] for n in range(6)], axis=0)
    return jnp.dot(jnp.concatenate(lhs, axis=1), rhs, preferred_element_type=f32)


def conv_back_pair(stack, outer, blocks, scene, p):
    total = None
    for j in range(3):
        for h in range(2):
            term = lax.dot_general(
                operand(stack, outer, scene, j, p + h),
                blocks[2 * j + 1 - h],
                (((1,), (1,)), ((), ())),
                preferred_element_type=f32,
            )
            total = term if total is None else total + term
    return total


def summed(pieces):
    total = pieces[0][...]
    for piece in pieces[1:]:
        total = total + piece[...]
    return total


def norm_stats(total, count):
    count = total[2:3] if count is None else count
    mean = total[0:1] / count
    inv = lax.rsqrt(total[1:2] / count - mean * mean + norm_eps)
    return mean, inv, count


def half_affine(mean, inv, gb):
    scale = inv * gb[0:1]
    return 0.5 * scale, 0.5 * (gb[1:2] - mean * scale)


def twice_slope(half, t):
    return (1.0 + t) + half * (1.0 - t * t)


def fold(value):
    return jnp.sum(value.reshape(-1, 8, value.shape[-1]), axis=0)


def plus(total, term):
    return term if total is None else total + term


def sum_rows(first, second, third=None):
    ch = first.shape[1]
    rows = [jnp.sum(first, axis=0, keepdims=True), jnp.sum(second, axis=0, keepdims=True)]
    rows.append(jnp.zeros((1, ch), f32) if third is None else third)
    return jnp.concatenate(rows + [jnp.zeros((5, ch), f32)], axis=0)


def put_parts(out, start, total):
    hi = total.astype(bf16).astype(f32)
    left = total - hi
    mid = left.astype(bf16).astype(f32)
    parts = [hi, mid, left - mid, jnp.zeros_like(total)]
    out[start : start + 16, :] = jnp.concatenate(parts[:2], axis=0).astype(bf16)
    out[start + 16 : start + 32, :] = jnp.concatenate(parts[2:], axis=0).astype(bf16)


def put_sums(sums, near, total):
    sums[...] = total
    if near is not None:
        put_parts(near, near.shape[0] - 32, total)


def mask_columns(rows):
    count, cols = rows.shape
    filled = jnp.concatenate([rows, jnp.zeros((128 - count, cols), f32)], axis=0)
    return filled.T


def mask_rows(place, mask):
    scenes, rows = mask.shape[1:3]
    parts = []
    for s in range(scenes):
        parts += [mask[place.section, s, pl.ds(place.row(q, rows), 1), :].astype(f32) for q in range(rows)]
    return jnp.concatenate(parts, axis=0)


def prep_kernel(mask, features, cot, weight, gain, bias, near, far, out, held, rows_mask, both, sems):
    place = Place()
    scenes, rows, cols, ch = features.shape[1:]
    half = weight.shape[1] // 2
    mine = pl.ds(pl.multiple_of(place.core * half, 16), half)
    moves = [
        (weight.at[0, mine], out.at[pl.ds(0, half)]),
        (gain, both.at[pl.ds(0, 1)]),
        (bias, both.at[pl.ds(1, 1)]),
        (mask.at[pl.ds(place.section, 1)], rows_mask),
    ]
    for source in (features, cot):
        for q in (0, rows - 1):
            moves.append((source.at[0, :, place.row(q, rows)], held.at[len(moves) - 4]))
    copies = [pltpu.make_async_copy(a, b, sems.at[n]) for n, (a, b) in enumerate(moves)]
    for copy in copies:
        copy.start()
    both[2:8] = jnp.zeros((6, ch), f32)
    for copy in copies:
        copy.wait()
    put_parts(out, half, both[...])
    parts = []
    for s in range(scenes):
        for q in (0, rows - 1):
            parts.append(rows_mask[0, s, pl.ds(place.row(q, rows), 1), :].astype(f32))
    columns = mask_columns(jnp.concatenate(parts, axis=0))
    size = scenes * cols
    for s in range(scenes):
        here = slice(s * cols, (s + 1) * cols)
        there = slice(size + s * cols, size + (s + 1) * cols)
        for n, edge in enumerate((near, far)):
            at = 2 * s + n
            edge[here, :] = (held[n, s].astype(f32) * columns[:, at : at + 1]).astype(bf16)
            edge[there, :] = held[2 + n, s]


def gather_kernel(own, gain, bias, r1, r2, r3, other, weights, gbs):
    place = Place()
    taps, ch = own.shape[1:]
    piece = taps // 6

    def put(section, p, rows):
        at = (2 * place.tap(p // 2) + p % 2) * piece
        weights[section, pl.ds(pl.multiple_of(at, 16), piece), :] = rows

    for p in range(6):
        put(place.section, p, own[0, p * piece : (p + 1) * piece])
    gbs[place.section] = jnp.concatenate([gain[...], bias[...], jnp.zeros((6, ch), f32)], axis=0)
    for d, got in ((1, r1), (2, r2), (3, r3)):
        there = place.section ^ d
        for n in range(3):
            rows = slice(n * piece, (n + 1) * piece)
            put(there, 3 * place.core + n, got[rows])
            put(there, 3 * (1 - place.core) + n, other[d - 1, rows])
        parts = got[3 * piece :].astype(f32)
        gbs[there] = parts[0:8] + parts[8:16] + parts[16:24]


def far_kernel(rows_ref, far):
    scenes, rows, cols, ch = rows_ref.shape
    for s in range(scenes):
        far[s * cols : (s + 1) * cols, :] = rows_ref[s, rows - 1].astype(bf16)


def finish_forward(stack, blocks, pre, near, sums, make_rows, columns, third):
    scenes, rows, cols, ch = pre.shape
    first = second = None
    make_rows(0)
    for scene in range(scenes):
        if scene + 1 < scenes:
            make_rows(scene + 1)
        for p in range(rows // 2):
            both = conv_pair(stack, None, blocks, scene, p)
            for n in range(2):
                r = 2 * p + n
                kept = row = both[:, n * ch : (n + 1) * ch]
                if columns is not None:
                    at = scene * rows + r
                    inside = columns[:, at : at + 1] > 0.5
                    kept = jnp.where(inside, row, hole)
                    row = jnp.where(inside, row, 0.0)
                pre[scene, r] = kept
                if r == 0:
                    near[scene * cols : (scene + 1) * cols, :] = kept.astype(bf16)
                first = plus(first, fold(row))
                second = plus(second, fold(row * row))
    put_sums(sums, near, sum_rows(first, second, third))


def first_kernel(mask, features, near, far, weights, x, pre, near_out, sums, stack, blocks):
    scenes, rows, cols, ch = features.shape[1:]
    put_blocks(weights.at[0], blocks)
    place = Place()
    mask_now = mask_rows(place, mask)
    columns = mask_columns(mask_now)

    def make_rows(scene):
        here = slice(scene * cols, (scene + 1) * cols)
        for k in range(rows + 2):
            if k == 0:
                value = near[here, :].astype(f32)
            elif k == rows + 1:
                value = far[here, :].astype(f32)
            else:
                at = scene * rows + k - 1
                value = features[0, scene, place.row(k - 1, rows)].astype(f32) * columns[:, at : at + 1]
            x[scene, k] = value.astype(bf16)
            put_row(stack, scene, k, value, False)

    total = jnp.sum(jnp.sum(mask_now, axis=1, keepdims=True), axis=0, keepdims=True)
    third = jnp.broadcast_to(total, (1, ch))
    finish_forward(stack, blocks, pre, near_out, sums, make_rows, columns, third)


def next_kernel(section, count, n, x_in, pre_in, near, far, *rest):
    pieces, rest = rest[:n], rest[n:]
    gbs, weights, x, pre, near_out, sums, stack, blocks = rest
    scenes, rows, cols, ch = pre.shape
    put_blocks(weights.at[section], blocks)
    scale, offset = stat_affine(pieces, count, gbs[section - 1])
    inside = Place().inside

    def make_rows(scene):
        here = slice(scene * cols, (scene + 1) * cols)
        for k in range(rows + 2):
            if k == 0:
                act = act_of(near[here, :].astype(f32), scale, offset, count)
            elif k == rows + 1:
                act = inside * act_of(far[here, :].astype(f32), scale, offset, count)
            else:
                act = act_of(pre_in[scene, k - 1], scale, offset, count)
            value = x_in[scene, k].astype(f32) + act
            x[scene, k] = value.astype(bf16)
            put_row(stack, scene, k, value, False)

    finish_forward(stack, blocks, pre, near_out, sums, make_rows, None, None)


def stat_affine(pieces, count, gb):
    mean, inv, _ = norm_stats(summed(pieces), count)
    return half_affine(mean, inv, gb)


def act_of(value, scale, offset, count):
    half = value * scale + offset
    act = half * jnp.tanh(half) + half
    return jnp.where(value > hole_edge, act, 0.0) if count is None else act


def slope_of(value, scale, offset, count):
    half = value * scale + offset
    out = twice_slope(half, jnp.tanh(half))
    return jnp.where(value > hole_edge, out, 0.0) if count is None else out


def at_scene(scene, cols):
    start = scene * cols
    return pl.ds(start if isinstance(scene, int) else pl.multiple_of(start, 16), cols)


def slope_kernel(section, count, n, pre, near, *rest):
    pieces, (gbs, slope) = rest[:n], rest[n:]
    scenes, padded, cols, ch = slope.shape
    scale, offset = stat_affine(pieces, count, gbs[section])

    @pl.loop(0, scenes)
    def _(scene):
        for k in range(padded):
            value = pre[scene, k - 1] if k else near[at_scene(scene, cols), :].astype(f32)
            slope[scene, k] = slope_of(value, scale, offset, count)


def turn_kernel(count, n, section, pre, cot, *rest):
    pieces, (gbs, grad_u, sums) = rest[:n], rest[n:]
    scenes, rows, cols, ch = grad_u.shape
    mean, inv, _ = norm_stats(summed(pieces), count)
    scale, offset = half_affine(mean, inv, gbs[section])
    place = Place()

    def one(scene, total):
        first, second = total
        for q in range(rows):
            value = pre[scene, q]
            grad = cot[0, scene, place.row(q, rows)].astype(f32) * slope_of(value, scale, offset, count)
            grad_u[scene, q] = grad
            first = first + fold(grad * value)
            second = second + fold(grad)
        return first, second

    zero = jnp.zeros((8, ch), f32)
    first, second = lax.fori_loop(0, scenes, one, (zero, zero))
    put_sums(sums, None, grad_sums(first, second, mean, inv))


def grad_sums(by_pre, plain, mean, inv):
    by_pre = 0.5 * jnp.sum(by_pre, axis=0, keepdims=True)
    plain = 0.5 * jnp.sum(plain, axis=0, keepdims=True)
    return jnp.concatenate(
        [inv * (by_pre - mean * plain), plain, jnp.zeros((6, plain.shape[1]), f32)], axis=0
    )


def neck_kernel(count, n, section, x, pre, *rest):
    pieces, (gbs, neck) = rest[:n], rest[n:]
    scenes, rows = neck.shape[1:3]
    scale, offset = stat_affine(pieces, count, gbs[section])
    place = Place()

    @pl.loop(0, scenes)
    def _(scene):
        for q in range(rows):
            act = act_of(pre[scene, q], scale, offset, count)
            neck[0, scene, place.row(q, rows)] = (x[scene, q + 1].astype(f32) + act).astype(bf16)


def back_terms(section, count, pieces, grads, gbs):
    mean, inv, cells = norm_stats(summed(pieces), count)
    total = summed(grads)
    lead = inv * gbs[section][0:1]
    by_pre = -lead * inv * total[0:1] / cells
    constant = -lead * total[1:2] / cells - by_pre * mean
    return (0.5 * lead, by_pre, constant), total


def grad_pre(terms, lifted, value, count):
    lead, by_pre, constant = terms
    out = lead * lifted + (by_pre * value + constant)
    return jnp.where(value > hole_edge, out, 0.0) if count is None else out


def back_rows(count, last, terms, stack, grad_u, g1, pre, p1, slope):
    scenes, rows, cols, ch = grad_u.shape
    base = scenes * cols if last else 0

    def make_rows(scene):
        at = scene * cols
        for k in range(rows + 1):
            if k:
                value = pre[scene, k - 1]
                lifted = grad_u[scene, k - 1]
            else:
                value = p1[at : at + cols, :].astype(f32)
                lifted = g1[base + at : base + at + cols, :].astype(f32) * slope[scene, 0]
            put_row(stack, scene, k, grad_pre(terms, lifted, value, count), True)

    return make_rows


def back_outer_row(section, count, last, terms, g2, p2, pieces, gbs, cols):
    base = p2.shape[0] if last else 0
    scale, offset = stat_affine(pieces, count, gbs[section])
    inside = Place().inside

    def outer_row(scene):
        at = at_scene(scene, cols)
        value = p2[at, :].astype(f32)
        lifted = g2[pl.ds(base + at.start, cols), :].astype(f32) * slope_of(value, scale, offset, count)
        return inside * grad_pre(terms, lifted, value, count)

    return outer_row


def grad_row(grad_in, last, scene, q, rows):
    return grad_in[0, scene, Place().row(q, rows)] if last else grad_in[scene, q]


def back_kernel(section, count, count_below, last, n, *rest):
    pieces, rest = rest[:n], rest[n:]
    grads, rest = rest[:n], rest[n:]
    pieces_below, rest = rest[:n], rest[n:]
    pre_below, slope_below, grad_u, grad_in, g1, g2, pre, p1, p2, slope, gbs, weights, *rest = rest
    stack, grad_out, grad_u_below, near, sums, total_out, blocks = rest
    scenes, rows, cols, ch = grad_u.shape
    put_blocks(weights.at[section], blocks)
    terms, total = back_terms(section, count, pieces, grads, gbs)
    total_out[...] = total
    mean_below, inv_below, _ = norm_stats(summed(pieces_below), count_below)
    make_rows = back_rows(count, last, terms, stack, grad_u, g1, pre, p1, slope)
    outer_row = back_outer_row(section, count, last, terms, g2, p2, pieces, gbs, cols)

    def make_all(scene):
        make_rows(scene)
        put_row(stack, scene, rows + 1, outer_row(scene), True)

    first = second = None
    make_all(0)
    for scene in range(scenes):
        if scene + 1 < scenes:
            make_all(scene + 1)
        for p in range(rows // 2):
            both = conv_back_pair(stack, None, blocks, scene, p)
            for m in range(2):
                r = 2 * p + m
                grad = grad_row(grad_in, last, scene, r, rows).astype(f32)
                grad = (grad + both[:, m * ch : (m + 1) * ch]).astype(bf16)
                grad_out[scene, r] = grad
                if r == 0:
                    near[scene * cols : (scene + 1) * cols, :] = grad
                lifted = grad.astype(f32) * slope_below[scene, r + 1]
                grad_u_below[scene, r] = lifted
                first = plus(first, fold(lifted * pre_below[scene, r]))
                second = plus(second, fold(lifted))
    put_sums(sums, near, grad_sums(first, second, mean_below, inv_below))


def final_weight_kernel(section, count, last, n, *rest):
    pieces, rest = rest[:n], rest[n:]
    grads, rest = rest[:n], rest[n:]
    grad_u, g1, pre, p1, slope, gbs, x, stack, mine, theirs, total_out, whole = rest
    terms, total = back_terms(section, count, pieces, grads, gbs)
    total_out[...] = total
    make_rows = back_rows(count, last, terms, stack, grad_u, g1, pre, p1, slope)
    weight_body(x, stack, mine, theirs, whole, make_rows)


def final_grad_kernel(section, count, last, n, *rest):
    pieces, rest = rest[:n], rest[n:]
    grads, rest = rest[:n], rest[n:]
    grad_in, g2, pre, p2, gbs, weights, stack, grad_out, outer, blocks = rest
    scenes, rows, cols, ch = grad_out.shape[1:]
    put_blocks(weights.at[section], blocks)
    terms, _ = back_terms(section, count, pieces, grads, gbs)
    outer_row = back_outer_row(section, count, last, terms, g2, p2, pieces, gbs, cols)
    place = Place()

    @pl.loop(0, scenes)
    def _(scene):
        put_outer(outer, scene, outer_row(scene), True)
        for p in range(rows // 2):
            both = conv_back_pair(stack, outer, blocks, scene, p)
            for m in range(2):
                r = 2 * p + m
                grad = grad_row(grad_in, last, scene, r, rows).astype(f32)
                grad = grad + both[:, m * ch : (m + 1) * ch]
                if count is None:
                    grad = jnp.where(pre[scene, r] > hole_edge, grad, 0.0)
                grad_out[0, scene, place.row(r, rows)] = grad.astype(bf16)


def weight_kernel(x, stack, mine, theirs, whole):
    weight_body(x, stack, mine, theirs, whole, None)


def weight_body(x, stack, mine, theirs, whole, make_rows):
    scenes, padded, cols, ch = x.shape
    rows = padded - 2
    place = Place()
    total = None
    if make_rows:
        make_rows(0)
    for scene in range(scenes):
        if make_rows and scene + 1 < scenes:
            make_rows(scene + 1)
        lines = [x[scene, k] for k in range(rows + 2)]
        lhs = jnp.concatenate(
            [jnp.concatenate(lines[i : i + rows], axis=0) for i in range(3)], axis=1
        )
        rhs = jnp.concatenate(
            [
                jnp.concatenate(
                    [
                        stack[j, k // 2, scene, :, (k % 2) * ch : (k % 2 + 1) * ch]
                        for j in range(3)
                    ],
                    axis=1,
                )
                for k in range(1, rows + 1)
            ],
            axis=0,
        )
        term = lax.dot_general(lhs, rhs, (((0,), (0,)), ((), ())), preferred_element_type=f32)
        total = plus(total, term)
    for i in range(3):
        for j in range(3):
            at = pl.multiple_of((3 * place.tap(i) + j) * ch, 8)
            whole[pl.ds(at, ch), :] = total[i * ch : (i + 1) * ch, j * ch : (j + 1) * ch]
    chips, chunk = mine.shape[:2]
    for z in range(chips):
        at = pl.multiple_of((2 * z + place.core) * chunk, 8)
        mine[z] = whole[pl.ds(at, chunk), :]
        at = pl.multiple_of((2 * z + 1 - place.core) * chunk, 8)
        theirs[z] = whole[pl.ds(at, chunk), :].astype(bf16)


def chip_kernel(n, *refs):
    mine, refs = refs[:n], refs[n:]
    theirs, refs = refs[:n], refs[n:]
    totals, refs = refs[:n], refs[n:]
    outs, held, sums = refs[:4], refs[4], refs[5]
    here = Place().section
    chips, chunk, ch = mine[0].shape
    for s in range(n):
        for z in range(chips):
            held[s, z * chunk : (z + 1) * chunk] = mine[s][z] + theirs[s][z].astype(f32)
        sums[s] = totals[s][...]
    size = chips * chunk
    for d in range(4):
        if d:
            outs[d][:size] = held[here ^ d].astype(bf16)
            put_parts(outs[d], size, sums[here ^ d])
        else:
            outs[0][:size] = held[here]
            outs[0][size:] = sums[here]


def section_kernel(own, a, b, c, mine, one, two, three, sums, held):
    chips, chunk = held.shape[:2]
    size = chips * chunk
    for z in range(chips):
        at = slice(z * chunk, (z + 1) * chunk)
        held[z] = own[at] + a[at].astype(f32) + b[at].astype(f32) + c[at].astype(f32)
    total = own[size:]
    for got in (a, b, c):
        parts = got[size:].astype(f32)
        total = total + (parts[0:8] + parts[8:16] + parts[16:24])
    sums[...] = total
    chip = Place().chip
    mine[...] = held[chip]
    for k, out in ((1, one), (2, two), (3, three)):
        out[...] = held[chip ^ k].astype(bf16)


def last_kernel(mine, a, b, c, sums, weight, gain, bias):
    gain[...] = sums[0:1]
    bias[...] = sums[1:2]
    weight[0] = mine[...] + a[...].astype(f32) + b[...].astype(f32) + c[...].astype(f32)


def call(body, outs, ins, scratch=(), flops=0, name=None, hbm=()):
    specs = [VMEM_SPEC] * len(ins)
    for n in hbm:
        specs[n] = pl.BlockSpec(memory_space=pltpu.HBM)
    return pl.pallas_call(
        body,
        out_shape=[jax.ShapeDtypeStruct(s, d) for s, d in outs],
        in_specs=specs,
        out_specs=[VMEM_SPEC] * len(outs),
        scratch_shapes=list(scratch),
        compiler_params=pltpu.CompilerParams(vmem_limit_bytes=12 * 2**20),
        cost_estimate=pl.CostEstimate(flops=flops, bytes_accessed=0, transcendentals=0),
        name=name,
    )(*ins)


def swap(value, axis, step):
    count = lax.axis_size(axis)
    return lax.ppermute(value, axis, [(i, i ^ step) for i in range(count)])


def swap_next(value):
    pairs = []
    for i in range(1, lax.axis_size("row") - 1, 2):
        pairs += [(i, i + 1), (i + 1, i)]
    return lax.ppermute(value, "row", pairs)


def row_pieces(total):
    count = lax.axis_size("row")
    stride = 2
    while True:
        group = min(4, count // stride)
        pieces = [total] + [swap(total, "row", k * stride) for k in range(1, group)]
        stride *= group
        if stride >= count:
            return pieces
        total = sum(pieces[1:], pieces[0])


def after(value, signal):
    return lax.optimization_barrier((value, signal))[0]


def far_rows(rows_ref):
    scenes, _, cols, ch = rows_ref.shape
    (far,) = call(far_kernel, [((scenes * cols, ch), bf16)], (rows_ref,), name="far")
    return far


def exchange(sums, near, rows_ref):
    got = swap(near, "row", 1)
    far = swap_next(far_rows(rows_ref))
    parts = got[got.shape[0] - 32 :].astype(f32)
    total = sums + (parts[0:8] + parts[8:16] + parts[16:24])
    return got, far, row_pieces(total), total


def per_device(features, conv_weight, norm_gain, norm_bias, valid_mask, out_cotangent):
    sections = lax.axis_size("section")
    tiles = lax.axis_size("row")
    scenes, rows, cols, ch = features.shape[1:]
    taps = conv_weight.shape[1]
    cells = float(scenes * rows * cols * tiles)
    tile_shape = (scenes, rows, cols, ch)
    pad_shape = (scenes, rows + 2, cols, ch)
    slope_shape = (scenes, rows + 1, cols, ch)
    edge = scenes * cols
    near_shape = (edge + 32, ch)
    sum_shape = (8, ch)
    stack_shape = (3, rows // 2 + 1, scenes, cols, 2 * ch)
    blocks = pltpu.VMEM((6, 2 * ch, 2 * ch), bf16)
    outer = pltpu.VMEM((3, scenes, cols, ch), bf16)
    flops = 2 * scenes * rows * cols * taps * ch
    half = taps // 2
    chunk = taps // tiles
    direct = tiles == 8 and chunk % 16 == 0

    def in_hbm(*values):
        return [pltpu.with_memory_space_constraint(v, pltpu.HBM) for v in values]

    e1, e2, wsend = call(
        prep_kernel,
        [((2 * edge, ch), bf16), ((2 * edge, ch), bf16), ((half + 32, ch), bf16)],
        in_hbm(valid_mask, features, out_cotangent, conv_weight, norm_gain, norm_bias),
        [
            pltpu.VMEM((4, scenes, cols, ch), bf16),
            pltpu.VMEM((1, scenes, rows, cols), jnp.int32),
            pltpu.VMEM((8, ch), f32),
            pltpu.SemaphoreType.DMA((8,)),
        ],
        hbm=range(6),
        name="prep",
    )
    got = [swap(wsend, "section", d) for d in (1, 2, 3)]
    e1 = swap(e1, "row", 1)
    e2 = swap_next(e2)
    got[1] = after(got[1], e1)
    other = swap(jnp.stack(got), "row", 1)
    weights, gbs = call(
        gather_kernel,
        [((sections, taps, ch), bf16), ((sections, 8, ch), f32)],
        (conv_weight, norm_gain, norm_bias, *got, other),
        name="gather",
    )

    forward_outs = [(pad_shape, bf16), (tile_shape, f32), (near_shape, bf16), (sum_shape, f32)]
    scratch = [pltpu.VMEM(stack_shape, bf16), blocks]
    kept = []
    slopes = []
    x, pre, near, sums = call(
        first_kernel,
        forward_outs,
        (valid_mask, features, e1, e2, weights),
        scratch,
        flops=flops,
        name="forward",
    )
    for section in range(sections):
        count = None if section == 0 else cells
        near, far, pieces, total = exchange(sums, near, pre)
        if section > 0:
            _, below, below_near, _, below_pieces, below_count = kept[-1]
            slopes += call(
                functools.partial(slope_kernel, section - 1, below_count, len(pieces)),
                [(slope_shape, f32)],
                (after(below, total), below_near, *below_pieces, gbs),
                name="slope",
            )
            pieces[0] = after(pieces[0], slopes[-1])
        kept.append((x, pre, near, far, pieces, count))
        if section == sections - 1:
            break
        x, pre, near, sums = call(
            functools.partial(next_kernel, section + 1, count, len(pieces)),
            forward_outs,
            (x, pre, near, far, *pieces, gbs, weights),
            scratch,
            flops=flops,
            name="forward",
        )
    n = len(pieces)
    grad_u, sums = call(
        functools.partial(turn_kernel, count, n, sections - 1),
        [(tile_shape, f32), (sum_shape, f32)],
        (pre, out_cotangent, *pieces, gbs),
        name="turn",
    )
    total = sums + swap(sums, "row", 1)
    grads = row_pieces(total)
    slopes += call(
        functools.partial(slope_kernel, sections - 1, count, n),
        [(slope_shape, f32)],
        (after(pre, total), near, *pieces, gbs),
        name="slope",
    )
    grad, g1, g2 = out_cotangent, e1, e2
    parts = [None] * sections
    totals = [None] * sections
    part_shapes = [((tiles // 2, chunk, ch), f32), ((tiles // 2, chunk, ch), bf16)]
    whole = pltpu.VMEM((taps, ch), f32)
    for section in range(sections - 1, 0, -1):
        x, pre, p1, p2, pieces, count = kept[section]
        _, below, _, _, below_pieces, below_count = kept[section - 1]
        last = section == sections - 1
        stack, grad, grad_u, near, sums, totals[section] = call(
            functools.partial(back_kernel, section, count, below_count, last, n),
            [
                (stack_shape, bf16),
                (tile_shape, bf16),
                (tile_shape, f32),
                (near_shape, bf16),
                (sum_shape, f32),
                (sum_shape, f32),
            ],
            (
                *pieces,
                *grads,
                *below_pieces,
                below,
                slopes[section - 1],
                grad_u,
                grad,
                g1,
                g2,
                pre,
                p1,
                p2,
                slopes[section],
                gbs,
                weights,
            ),
            [blocks],
            flops=flops,
            name="backward",
        )
        g1, g2, grads, total = exchange(sums, near, grad)
        parts[section] = call(
            weight_kernel,
            part_shapes,
            (x, after(stack, total)),
            [whole],
            flops=flops,
            name="weight",
        )
        grads[0] = after(grads[0], parts[section][1])
    x, pre, p1, p2, pieces, count = kept[0]
    last = sections == 1
    stack, *parts[0], totals[0] = call(
        functools.partial(final_weight_kernel, 0, count, last, n),
        [(stack_shape, bf16), *part_shapes, (sum_shape, f32)],
        (*pieces, *grads, grad_u, g1, pre, p1, slopes[0], gbs, x),
        [whole],
        flops=flops,
        name="weight",
    )

    def finish(signal):
        (feature_grad,) = call(
            functools.partial(final_grad_kernel, 0, count, last, n),
            [((1,) + tile_shape, bf16)],
            (*pieces, *grads, grad, g2, pre, p2, gbs, weights, after(stack, signal)),
            [outer, blocks],
            flops=flops,
            name="final_grad",
        )
        last_x, last_pre, _, _, last_pieces, last_count = kept[-1]
        (neck,) = call(
            functools.partial(neck_kernel, last_count, n, sections - 1),
            [((1,) + tile_shape, bf16)],
            (last_x, after(last_pre, signal), *last_pieces, gbs),
            flops=flops,
            name="neck",
        )
        return neck, feature_grad

    m = sections
    if direct:
        size = taps // 2
        theirs = [swap(p[1], "row", 1) for p in parts]
        own, *sending = call(
            functools.partial(chip_kernel, m),
            [((size + 8, ch), f32)] + [((size + 32, ch), bf16)] * 3,
            (*[p[0] for p in parts], *theirs, *totals),
            [pltpu.VMEM((m, size, ch), f32), pltpu.VMEM((m, 8, ch), f32)],
            name="chips",
        )
        received = [swap(v, "section", d + 1) for d, v in enumerate(sending)]
        neck, feature_grad = finish(own)
        received[0] = after(received[0], (neck, feature_grad))
        mine, one, two, three, total = call(
            section_kernel,
            [((chunk, ch), f32)] + [((chunk, ch), bf16)] * 3 + [(sum_shape, f32)],
            (own, *received),
            [pltpu.VMEM((tiles // 2, chunk, ch), f32)],
            name="sections",
        )
        chunks = [swap(v, "row", 2 * (k + 1)) for k, v in enumerate((one, two, three))]
        weight_grad, gain_grad, bias_grad = call(
            last_kernel,
            [((1, chunk, ch), f32), ((1, ch), f32), ((1, ch), f32)],
            (mine, *chunks, total),
            name="last",
        )
    else:
        lanes = [list(range(c, tiles, 2)) for c in range(2)]
        here = lax.axis_index("section")
        chip_sums = jnp.stack([p[0] + swap(p[1], "row", 1).astype(f32) for p in parts])
        sums = jnp.stack(totals)

        def over_sections(stacked):
            total, *others = [
                lax.dynamic_index_in_dim(stacked, here ^ d, 0, keepdims=False) for d in range(4)
            ]
            for d, other in enumerate(others):
                total = total + swap(other, "section", d + 1)
            return total

        chip_sum, total = over_sections(chip_sums), over_sections(sums)
        weight_grad = lax.psum_scatter(
            chip_sum, "row", scatter_dimension=0, tiled=True, axis_index_groups=lanes
        )
        gain_grad, bias_grad = total[0:1], total[1:2]
        neck, feature_grad = finish(total)
    return neck, feature_grad, weight_grad, gain_grad, bias_grad


def solution(mesh):
    return jax.shard_map(
        per_device,
        mesh=mesh,
        in_specs=(
            P("section", None, "row", None, None),
            P("section", None, None),
            P("section", None),
            P("section", None),
            P(None, None, "row", None),
            P("section", None, "row", None, None),
        ),
        out_specs=(
            P("section", None, "row", None, None),
            P("section", None, "row", None, None),
            P("section", "row", None),
            P("section", None),
            P("section", None),
        ),
        check_vma=False,
    )
```

```python
import functools

import jax
import jax.numpy as jnp
from jax import lax
from jax.experimental import pallas as pl
from jax.experimental.pallas import tpu as pltpu
from jax.sharding import PartitionSpec as P

norm_eps = 1e-05
hole = -1e30
hole_edge = -1e29
f32 = jnp.float32
bf16 = jnp.bfloat16
VMEM_SPEC = pl.BlockSpec(memory_space=pltpu.VMEM)


class Place:
    def __init__(self):
        tile = lax.axis_index("row")
        self.section = lax.axis_index("section")
        self.core = lax.rem(tile, 2)
        self.even = self.core == 0
        self.chip = tile // 2
        outer = jnp.where(self.even, 0, lax.axis_size("row") - 1)
        self.inside = (tile != outer).astype(f32)

    def row(self, q, rows):
        return jnp.where(self.even, rows - 1 - q, q)

    def tap(self, i):
        return jnp.where(self.even, 2 - i, i)


def shifted(value, step):
    cols = value.shape[0]
    index = lax.broadcasted_iota(jnp.int32, value.shape, 0)
    edge = 0 if step == 1 else cols - 1
    return jnp.where(index == edge, 0.0, pltpu.roll(value, step % cols, 0))


def shifts(value, flip):
    left, right = shifted(value, 1).astype(bf16), shifted(value, -1).astype(bf16)
    return (right, value.astype(bf16), left) if flip else (left, value.astype(bf16), right)


def put_row(stack, scene, k, value, flip):
    ch = value.shape[1]
    for j, part in enumerate(shifts(value, flip)):
        stack[j, k // 2, scene, :, (k % 2) * ch : (k % 2 + 1) * ch] = part


def put_outer(outer, scene, value, flip):
    for j, part in enumerate(shifts(value, flip)):
        outer[j, scene] = part


def put_blocks(kernel_rows, blocks):
    ch = kernel_rows.shape[1]

    def tap(i, j):
        return kernel_rows[(3 * i + j) * ch : (3 * i + j + 1) * ch, :]

    zero = jnp.zeros((ch, ch), bf16)
    for j in range(3):
        blocks[2 * j, :ch, :ch] = tap(0, j)
        blocks[2 * j, :ch, ch:] = zero
        blocks[2 * j, ch:, :ch] = tap(1, j)
        blocks[2 * j, ch:, ch:] = tap(0, j)
        blocks[2 * j + 1, :ch, :ch] = tap(2, j)
        blocks[2 * j + 1, :ch, ch:] = tap(1, j)
        blocks[2 * j + 1, ch:, :ch] = zero
        blocks[2 * j + 1, ch:, ch:] = tap(2, j)


def operand(stack, outer, scene, j, pair):
    if outer is None or pair + 1 < stack.shape[1]:
        return stack[j, pair, scene]
    ch = outer.shape[-1]
    return jnp.concatenate([stack[j, pair, scene, :, :ch], outer[j, scene]], axis=1)


def conv_pair(stack, outer, blocks, scene, p):
    lhs = [operand(stack, outer, scene, j, p + h) for j in range(3) for h in range(2)]
    rhs = jnp.concatenate([blocks[n] for n in range(6)], axis=0)
    return jnp.dot(jnp.concatenate(lhs, axis=1), rhs, preferred_element_type=f32)


def conv_back_pair(stack, outer, blocks, scene, p):
    total = None
    for j in range(3):
        for h in range(2):
            term = lax.dot_general(
                operand(stack, outer, scene, j, p + h),
                blocks[2 * j + 1 - h],
                (((1,), (1,)), ((), ())),
                preferred_element_type=f32,
            )
            total = term if total is None else total + term
    return total


def summed(pieces):
    total = pieces[0][...]
    for piece in pieces[1:]:
        total = total + piece[...]
    return total


def norm_stats(total, count):
    count = total[2:3] if count is None else count
    mean = total[0:1] / count
    inv = lax.rsqrt(total[1:2] / count - mean * mean + norm_eps)
    return mean, inv, count


def half_affine(mean, inv, gb):
    scale = inv * gb[0:1]
    return 0.5 * scale, 0.5 * (gb[1:2] - mean * scale)


def twice_slope(half, t):
    return (1.0 + t) + half * (1.0 - t * t)


def fold(value):
    return jnp.sum(value.reshape(-1, 8, value.shape[-1]), axis=0)


def plus(total, term):
    return term if total is None else total + term


def sum_rows(first, second, third=None):
    ch = first.shape[1]
    rows = [jnp.sum(first, axis=0, keepdims=True), jnp.sum(second, axis=0, keepdims=True)]
    rows.append(jnp.zeros((1, ch), f32) if third is None else third)
    return jnp.concatenate(rows + [jnp.zeros((5, ch), f32)], axis=0)


def put_parts(out, start, total):
    hi = total.astype(bf16).astype(f32)
    left = total - hi
    mid = left.astype(bf16).astype(f32)
    parts = [hi, mid, left - mid, jnp.zeros_like(total)]
    out[start : start + 16, :] = jnp.concatenate(parts[:2], axis=0).astype(bf16)
    out[start + 16 : start + 32, :] = jnp.concatenate(parts[2:], axis=0).astype(bf16)


def put_sums(sums, near, total):
    sums[...] = total
    if near is not None:
        put_parts(near, near.shape[0] - 32, total)


def mask_columns(rows):
    count, cols = rows.shape
    filled = jnp.concatenate([rows, jnp.zeros((128 - count, cols), f32)], axis=0)
    return filled.T


def mask_rows(place, mask):
    scenes, rows = mask.shape[1:3]
    parts = []
    for s in range(scenes):
        parts += [mask[place.section, s, pl.ds(place.row(q, rows), 1), :].astype(f32) for q in range(rows)]
    return jnp.concatenate(parts, axis=0)


def prep_kernel(mask, features, cot, weight, gain, bias, near, far, out, held, rows_mask, both, sems):
    place = Place()
    scenes, rows, cols, ch = features.shape[1:]
    half = weight.shape[1] // 2
    mine = pl.ds(pl.multiple_of(place.core * half, 16), half)
    moves = [
        (weight.at[0, mine], out.at[pl.ds(0, half)]),
        (gain, both.at[pl.ds(0, 1)]),
        (bias, both.at[pl.ds(1, 1)]),
        (mask.at[pl.ds(place.section, 1)], rows_mask),
    ]
    for source in (features, cot):
        for q in (0, rows - 1):
            moves.append((source.at[0, :, place.row(q, rows)], held.at[len(moves) - 4]))
    copies = [pltpu.make_async_copy(a, b, sems.at[n]) for n, (a, b) in enumerate(moves)]
    for copy in copies:
        copy.start()
    both[2:8] = jnp.zeros((6, ch), f32)
    for copy in copies:
        copy.wait()
    put_parts(out, half, both[...])
    parts = []
    for s in range(scenes):
        for q in (0, rows - 1):
            parts.append(rows_mask[0, s, pl.ds(place.row(q, rows), 1), :].astype(f32))
    columns = mask_columns(jnp.concatenate(parts, axis=0))
    size = scenes * cols
    for s in range(scenes):
        here = slice(s * cols, (s + 1) * cols)
        there = slice(size + s * cols, size + (s + 1) * cols)
        for n, edge in enumerate((near, far)):
            at = 2 * s + n
            edge[here, :] = (held[n, s].astype(f32) * columns[:, at : at + 1]).astype(bf16)
            edge[there, :] = held[2 + n, s]


def gather_kernel(own, gain, bias, r1, r2, r3, other, weights, gbs):
    place = Place()
    taps, ch = own.shape[1:]
    piece = taps // 6

    def put(section, p, rows):
        at = (2 * place.tap(p // 2) + p % 2) * piece
        weights[section, pl.ds(pl.multiple_of(at, 16), piece), :] = rows

    for p in range(6):
        put(place.section, p, own[0, p * piece : (p + 1) * piece])
    gbs[place.section] = jnp.concatenate([gain[...], bias[...], jnp.zeros((6, ch), f32)], axis=0)
    for d, got in ((1, r1), (2, r2), (3, r3)):
        there = place.section ^ d
        for n in range(3):
            rows = slice(n * piece, (n + 1) * piece)
            put(there, 3 * place.core + n, got[rows])
            put(there, 3 * (1 - place.core) + n, other[d - 1, rows])
        parts = got[3 * piece :].astype(f32)
        gbs[there] = parts[0:8] + parts[8:16] + parts[16:24]


def far_kernel(rows_ref, far):
    scenes, rows, cols, ch = rows_ref.shape
    for s in range(scenes):
        far[s * cols : (s + 1) * cols, :] = rows_ref[s, rows - 1].astype(bf16)


def finish_forward(stack, blocks, pre, near, sums, make_rows, columns, third):
    scenes, rows, cols, ch = pre.shape
    first = second = None
    make_rows(0)
    for scene in range(scenes):
        if scene + 1 < scenes:
            make_rows(scene + 1)
        for p in range(rows // 2):
            both = conv_pair(stack, None, blocks, scene, p)
            for n in range(2):
                r = 2 * p + n
                kept = row = both[:, n * ch : (n + 1) * ch]
                if columns is not None:
                    at = scene * rows + r
                    inside = columns[:, at : at + 1] > 0.5
                    kept = jnp.where(inside, row, hole)
                    row = jnp.where(inside, row, 0.0)
                pre[scene, r] = kept
                if r == 0:
                    near[scene * cols : (scene + 1) * cols, :] = kept.astype(bf16)
                first = plus(first, fold(row))
                second = plus(second, fold(row * row))
    put_sums(sums, near, sum_rows(first, second, third))


def first_kernel(mask, features, near, far, weights, x, pre, near_out, sums, stack, blocks):
    scenes, rows, cols, ch = features.shape[1:]
    put_blocks(weights.at[0], blocks)
    place = Place()
    mask_now = mask_rows(place, mask)
    columns = mask_columns(mask_now)

    def make_rows(scene):
        here = slice(scene * cols, (scene + 1) * cols)
        for k in range(rows + 2):
            if k == 0:
                value = near[here, :].astype(f32)
            elif k == rows + 1:
                value = far[here, :].astype(f32)
            else:
                at = scene * rows + k - 1
                value = features[0, scene, place.row(k - 1, rows)].astype(f32) * columns[:, at : at + 1]
            x[scene, k] = value.astype(bf16)
            put_row(stack, scene, k, value, False)

    total = jnp.sum(jnp.sum(mask_now, axis=1, keepdims=True), axis=0, keepdims=True)
    third = jnp.broadcast_to(total, (1, ch))
    finish_forward(stack, blocks, pre, near_out, sums, make_rows, columns, third)


def next_kernel(section, count, n, x_in, pre_in, near, far, *rest):
    pieces, rest = rest[:n], rest[n:]
    gbs, weights, x, pre, near_out, sums, stack, blocks = rest
    scenes, rows, cols, ch = pre.shape
    put_blocks(weights.at[section], blocks)
    scale, offset = stat_affine(pieces, count, gbs[section - 1])
    inside = Place().inside

    def make_rows(scene):
        here = slice(scene * cols, (scene + 1) * cols)
        for k in range(rows + 2):
            if k == 0:
                act = act_of(near[here, :].astype(f32), scale, offset, count)
            elif k == rows + 1:
                act = inside * act_of(far[here, :].astype(f32), scale, offset, count)
            else:
                act = act_of(pre_in[scene, k - 1], scale, offset, count)
            value = x_in[scene, k].astype(f32) + act
            x[scene, k] = value.astype(bf16)
            put_row(stack, scene, k, value, False)

    finish_forward(stack, blocks, pre, near_out, sums, make_rows, None, None)


def stat_affine(pieces, count, gb):
    mean, inv, _ = norm_stats(summed(pieces), count)
    return half_affine(mean, inv, gb)


def act_of(value, scale, offset, count):
    half = value * scale + offset
    act = half * jnp.tanh(half) + half
    return jnp.where(value > hole_edge, act, 0.0) if count is None else act


def slope_of(value, scale, offset, count):
    half = value * scale + offset
    out = twice_slope(half, jnp.tanh(half))
    return jnp.where(value > hole_edge, out, 0.0) if count is None else out


def at_scene(scene, cols):
    start = scene * cols
    return pl.ds(start if isinstance(scene, int) else pl.multiple_of(start, 16), cols)


def slope_kernel(section, count, n, pre, near, *rest):
    pieces, (gbs, slope) = rest[:n], rest[n:]
    scenes, padded, cols, ch = slope.shape
    scale, offset = stat_affine(pieces, count, gbs[section])

    @pl.loop(0, scenes)
    def _(scene):
        for k in range(padded):
            value = pre[scene, k - 1] if k else near[at_scene(scene, cols), :].astype(f32)
            slope[scene, k] = slope_of(value, scale, offset, count)


def turn_kernel(count, n, section, pre, cot, *rest):
    pieces, (gbs, grad_u, sums) = rest[:n], rest[n:]
    scenes, rows, cols, ch = grad_u.shape
    mean, inv, _ = norm_stats(summed(pieces), count)
    scale, offset = half_affine(mean, inv, gbs[section])
    place = Place()

    def one(scene, total):
        first, second = total
        for q in range(rows):
            value = pre[scene, q]
            grad = cot[0, scene, place.row(q, rows)].astype(f32) * slope_of(value, scale, offset, count)
            grad_u[scene, q] = grad
            first = first + fold(grad * value)
            second = second + fold(grad)
        return first, second

    zero = jnp.zeros((8, ch), f32)
    first, second = lax.fori_loop(0, scenes, one, (zero, zero))
    put_sums(sums, None, grad_sums(first, second, mean, inv))


def grad_sums(by_pre, plain, mean, inv):
    by_pre = 0.5 * jnp.sum(by_pre, axis=0, keepdims=True)
    plain = 0.5 * jnp.sum(plain, axis=0, keepdims=True)
    return jnp.concatenate(
        [inv * (by_pre - mean * plain), plain, jnp.zeros((6, plain.shape[1]), f32)], axis=0
    )


def neck_kernel(count, n, section, x, pre, *rest):
    pieces, (gbs, neck) = rest[:n], rest[n:]
    scenes, rows = neck.shape[1:3]
    scale, offset = stat_affine(pieces, count, gbs[section])
    place = Place()

    @pl.loop(0, scenes)
    def _(scene):
        for q in range(rows):
            act = act_of(pre[scene, q], scale, offset, count)
            neck[0, scene, place.row(q, rows)] = (x[scene, q + 1].astype(f32) + act).astype(bf16)


def back_terms(section, count, pieces, grads, gbs):
    mean, inv, cells = norm_stats(summed(pieces), count)
    total = summed(grads)
    lead = inv * gbs[section][0:1]
    by_pre = -lead * inv * total[0:1] / cells
    constant = -lead * total[1:2] / cells - by_pre * mean
    return (0.5 * lead, by_pre, constant), total


def grad_pre(terms, lifted, value, count):
    lead, by_pre, constant = terms
    out = lead * lifted + (by_pre * value + constant)
    return jnp.where(value > hole_edge, out, 0.0) if count is None else out


def back_rows(count, last, terms, stack, grad_u, g1, pre, p1, slope):
    scenes, rows, cols, ch = grad_u.shape
    base = scenes * cols if last else 0

    def make_rows(scene):
        at = scene * cols
        for k in range(rows + 1):
            if k:
                value = pre[scene, k - 1]
                lifted = grad_u[scene, k - 1]
            else:
                value = p1[at : at + cols, :].astype(f32)
                lifted = g1[base + at : base + at + cols, :].astype(f32) * slope[scene, 0]
            put_row(stack, scene, k, grad_pre(terms, lifted, value, count), True)

    return make_rows


def back_outer_row(section, count, last, terms, g2, p2, pieces, gbs, cols):
    base = p2.shape[0] if last else 0
    scale, offset = stat_affine(pieces, count, gbs[section])
    inside = Place().inside

    def outer_row(scene):
        at = at_scene(scene, cols)
        value = p2[at, :].astype(f32)
        lifted = g2[pl.ds(base + at.start, cols), :].astype(f32) * slope_of(value, scale, offset, count)
        return inside * grad_pre(terms, lifted, value, count)

    return outer_row


def grad_row(grad_in, last, scene, q, rows):
    return grad_in[0, scene, Place().row(q, rows)] if last else grad_in[scene, q]


def back_kernel(section, count, count_below, last, n, *rest):
    pieces, rest = rest[:n], rest[n:]
    grads, rest = rest[:n], rest[n:]
    pieces_below, rest = rest[:n], rest[n:]
    pre_below, slope_below, grad_u, grad_in, g1, g2, pre, p1, p2, slope, gbs, weights, *rest = rest
    stack, grad_out, grad_u_below, near, sums, total_out, blocks = rest
    scenes, rows, cols, ch = grad_u.shape
    put_blocks(weights.at[section], blocks)
    terms, total = back_terms(section, count, pieces, grads, gbs)
    total_out[...] = total
    mean_below, inv_below, _ = norm_stats(summed(pieces_below), count_below)
    make_rows = back_rows(count, last, terms, stack, grad_u, g1, pre, p1, slope)
    outer_row = back_outer_row(section, count, last, terms, g2, p2, pieces, gbs, cols)

    def make_all(scene):
        make_rows(scene)
        put_row(stack, scene, rows + 1, outer_row(scene), True)

    first = second = None
    make_all(0)
    for scene in range(scenes):
        if scene + 1 < scenes:
            make_all(scene + 1)
        for p in range(rows // 2):
            both = conv_back_pair(stack, None, blocks, scene, p)
            for m in range(2):
                r = 2 * p + m
                grad = grad_row(grad_in, last, scene, r, rows).astype(f32)
                grad = (grad + both[:, m * ch : (m + 1) * ch]).astype(bf16)
                grad_out[scene, r] = grad
                if r == 0:
                    near[scene * cols : (scene + 1) * cols, :] = grad
                lifted = grad.astype(f32) * slope_below[scene, r + 1]
                grad_u_below[scene, r] = lifted
                first = plus(first, fold(lifted * pre_below[scene, r]))
                second = plus(second, fold(lifted))
    put_sums(sums, near, grad_sums(first, second, mean_below, inv_below))


def final_weight_kernel(section, count, last, n, *rest):
    pieces, rest = rest[:n], rest[n:]
    grads, rest = rest[:n], rest[n:]
    grad_u, g1, pre, p1, slope, gbs, x, stack, mine, theirs, total_out, whole = rest
    terms, total = back_terms(section, count, pieces, grads, gbs)
    total_out[...] = total
    make_rows = back_rows(count, last, terms, stack, grad_u, g1, pre, p1, slope)
    weight_body(x, stack, mine, theirs, whole, make_rows)


def final_grad_kernel(section, count, last, n, *rest):
    pieces, rest = rest[:n], rest[n:]
    grads, rest = rest[:n], rest[n:]
    grad_in, g2, pre, p2, gbs, weights, stack, grad_out, outer, blocks = rest
    scenes, rows, cols, ch = grad_out.shape[1:]
    put_blocks(weights.at[section], blocks)
    terms, _ = back_terms(section, count, pieces, grads, gbs)
    outer_row = back_outer_row(section, count, last, terms, g2, p2, pieces, gbs, cols)
    place = Place()

    @pl.loop(0, scenes)
    def _(scene):
        put_outer(outer, scene, outer_row(scene), True)
        for p in range(rows // 2):
            both = conv_back_pair(stack, outer, blocks, scene, p)
            for m in range(2):
                r = 2 * p + m
                grad = grad_row(grad_in, last, scene, r, rows).astype(f32)
                grad = grad + both[:, m * ch : (m + 1) * ch]
                if count is None:
                    grad = jnp.where(pre[scene, r] > hole_edge, grad, 0.0)
                grad_out[0, scene, place.row(r, rows)] = grad.astype(bf16)


def weight_kernel(x, stack, mine, theirs, whole):
    weight_body(x, stack, mine, theirs, whole, None)


def weight_body(x, stack, mine, theirs, whole, make_rows):
    scenes, padded, cols, ch = x.shape
    rows = padded - 2
    place = Place()
    total = None
    if make_rows:
        make_rows(0)
    for scene in range(scenes):
        if make_rows and scene + 1 < scenes:
            make_rows(scene + 1)
        lines = [x[scene, k] for k in range(rows + 2)]
        lhs = jnp.concatenate(
            [jnp.concatenate(lines[i : i + rows], axis=0) for i in range(3)], axis=1
        )
        rhs = jnp.concatenate(
            [
                jnp.concatenate(
                    [
                        stack[j, k // 2, scene, :, (k % 2) * ch : (k % 2 + 1) * ch]
                        for j in range(3)
                    ],
                    axis=1,
                )
                for k in range(1, rows + 1)
            ],
            axis=0,
        )
        term = lax.dot_general(lhs, rhs, (((0,), (0,)), ((), ())), preferred_element_type=f32)
        total = plus(total, term)
    for i in range(3):
        for j in range(3):
            at = pl.multiple_of((3 * place.tap(i) + j) * ch, 8)
            whole[pl.ds(at, ch), :] = total[i * ch : (i + 1) * ch, j * ch : (j + 1) * ch]
    chips, chunk = mine.shape[:2]
    for z in range(chips):
        at = pl.multiple_of((2 * z + place.core) * chunk, 8)
        mine[z] = whole[pl.ds(at, chunk), :]
        at = pl.multiple_of((2 * z + 1 - place.core) * chunk, 8)
        theirs[z] = whole[pl.ds(at, chunk), :].astype(bf16)


def chip_kernel(n, *refs):
    mine, refs = refs[:n], refs[n:]
    theirs, refs = refs[:n], refs[n:]
    totals, refs = refs[:n], refs[n:]
    outs, held, sums = refs[:4], refs[4], refs[5]
    here = Place().section
    chips, chunk, ch = mine[0].shape
    for s in range(n):
        for z in range(chips):
            held[s, z * chunk : (z + 1) * chunk] = mine[s][z] + theirs[s][z].astype(f32)
        sums[s] = totals[s][...]
    size = chips * chunk
    for d in range(4):
        if d:
            outs[d][:size] = held[here ^ d].astype(bf16)
            put_parts(outs[d], size, sums[here ^ d])
        else:
            outs[0][:size] = held[here]
            outs[0][size:] = sums[here]


def section_kernel(own, a, b, c, mine, one, two, three, sums, held):
    chips, chunk = held.shape[:2]
    size = chips * chunk
    for z in range(chips):
        at = slice(z * chunk, (z + 1) * chunk)
        held[z] = own[at] + a[at].astype(f32) + b[at].astype(f32) + c[at].astype(f32)
    total = own[size:]
    for got in (a, b, c):
        parts = got[size:].astype(f32)
        total = total + (parts[0:8] + parts[8:16] + parts[16:24])
    sums[...] = total
    chip = Place().chip
    mine[...] = held[chip]
    for k, out in ((1, one), (2, two), (3, three)):
        out[...] = held[chip ^ k].astype(bf16)


def last_kernel(mine, a, b, c, sums, weight, gain, bias):
    gain[...] = sums[0:1]
    bias[...] = sums[1:2]
    weight[0] = mine[...] + a[...].astype(f32) + b[...].astype(f32) + c[...].astype(f32)


def call(body, outs, ins, scratch=(), flops=0, name=None, hbm=()):
    specs = [VMEM_SPEC] * len(ins)
    for n in hbm:
        specs[n] = pl.BlockSpec(memory_space=pltpu.HBM)
    return pl.pallas_call(
        body,
        out_shape=[jax.ShapeDtypeStruct(s, d) for s, d in outs],
        in_specs=specs,
        out_specs=[VMEM_SPEC] * len(outs),
        scratch_shapes=list(scratch),
        compiler_params=pltpu.CompilerParams(vmem_limit_bytes=12 * 2**20),
        cost_estimate=pl.CostEstimate(flops=flops, bytes_accessed=0, transcendentals=0),
        name=name,
    )(*ins)


def swap(value, axis, step):
    count = lax.axis_size(axis)
    return lax.ppermute(value, axis, [(i, i ^ step) for i in range(count)])


def swap_next(value):
    pairs = []
    for i in range(1, lax.axis_size("row") - 1, 2):
        pairs += [(i, i + 1), (i + 1, i)]
    return lax.ppermute(value, "row", pairs)


def row_pieces(total):
    count = lax.axis_size("row")
    stride = 2
    while True:
        group = min(4, count // stride)
        pieces = [total] + [swap(total, "row", k * stride + (stride == 2)) for k in range(1, group)]
        stride *= group
        if stride >= count:
            return pieces
        total = sum(pieces[1:], pieces[0])


def after(value, signal):
    return lax.optimization_barrier((value, signal))[0]


def far_rows(rows_ref):
    scenes, _, cols, ch = rows_ref.shape
    (far,) = call(far_kernel, [((scenes * cols, ch), bf16)], (rows_ref,), name="far")
    return far


def exchange(sums, near, rows_ref):
    got = swap(near, "row", 1)
    far = swap_next(far_rows(rows_ref))
    parts = got[got.shape[0] - 32 :].astype(f32)
    total = sums + (parts[0:8] + parts[8:16] + parts[16:24])
    return got, far, row_pieces(total), total


def per_device(features, conv_weight, norm_gain, norm_bias, valid_mask, out_cotangent):
    sections = lax.axis_size("section")
    tiles = lax.axis_size("row")
    scenes, rows, cols, ch = features.shape[1:]
    taps = conv_weight.shape[1]
    cells = float(scenes * rows * cols * tiles)
    tile_shape = (scenes, rows, cols, ch)
    pad_shape = (scenes, rows + 2, cols, ch)
    slope_shape = (scenes, rows + 1, cols, ch)
    edge = scenes * cols
    near_shape = (edge + 32, ch)
    sum_shape = (8, ch)
    stack_shape = (3, rows // 2 + 1, scenes, cols, 2 * ch)
    blocks = pltpu.VMEM((6, 2 * ch, 2 * ch), bf16)
    outer = pltpu.VMEM((3, scenes, cols, ch), bf16)
    flops = 2 * scenes * rows * cols * taps * ch
    half = taps // 2
    chunk = taps // tiles
    direct = tiles == 8 and chunk % 16 == 0

    def in_hbm(*values):
        return [pltpu.with_memory_space_constraint(v, pltpu.HBM) for v in values]

    e1, e2, wsend = call(
        prep_kernel,
        [((2 * edge, ch), bf16), ((2 * edge, ch), bf16), ((half + 32, ch), bf16)],
        in_hbm(valid_mask, features, out_cotangent, conv_weight, norm_gain, norm_bias),
        [
            pltpu.VMEM((4, scenes, cols, ch), bf16),
            pltpu.VMEM((1, scenes, rows, cols), jnp.int32),
            pltpu.VMEM((8, ch), f32),
            pltpu.SemaphoreType.DMA((8,)),
        ],
        hbm=range(6),
        name="prep",
    )
    got = [swap(wsend, "section", d) for d in (1, 2, 3)]
    e1 = swap(e1, "row", 1)
    e2 = swap_next(e2)
    got[1] = after(got[1], e1)
    other = swap(jnp.stack(got), "row", 1)
    weights, gbs = call(
        gather_kernel,
        [((sections, taps, ch), bf16), ((sections, 8, ch), f32)],
        (conv_weight, norm_gain, norm_bias, *got, other),
        name="gather",
    )

    forward_outs = [(pad_shape, bf16), (tile_shape, f32), (near_shape, bf16), (sum_shape, f32)]
    scratch = [pltpu.VMEM(stack_shape, bf16), blocks]
    kept = []
    slopes = []
    x, pre, near, sums = call(
        first_kernel,
        forward_outs,
        (valid_mask, features, e1, e2, weights),
        scratch,
        flops=flops,
        name="forward",
    )
    for section in range(sections):
        count = None if section == 0 else cells
        near, far, pieces, total = exchange(sums, near, pre)
        if section > 0:
            _, below, below_near, _, below_pieces, below_count = kept[-1]
            slopes += call(
                functools.partial(slope_kernel, section - 1, below_count, len(pieces)),
                [(slope_shape, f32)],
                (after(below, total), below_near, *below_pieces, gbs),
                name="slope",
            )
            pieces[0] = after(pieces[0], slopes[-1])
        kept.append((x, pre, near, far, pieces, count))
        if section == sections - 1:
            break
        x, pre, near, sums = call(
            functools.partial(next_kernel, section + 1, count, len(pieces)),
            forward_outs,
            (x, pre, near, far, *pieces, gbs, weights),
            scratch,
            flops=flops,
            name="forward",
        )
    n = len(pieces)
    grad_u, sums = call(
        functools.partial(turn_kernel, count, n, sections - 1),
        [(tile_shape, f32), (sum_shape, f32)],
        (pre, out_cotangent, *pieces, gbs),
        name="turn",
    )
    total = sums + swap(sums, "row", 1)
    grads = row_pieces(total)
    slopes += call(
        functools.partial(slope_kernel, sections - 1, count, n),
        [(slope_shape, f32)],
        (after(pre, total), near, *pieces, gbs),
        name="slope",
    )
    grad, g1, g2 = out_cotangent, e1, e2
    parts = [None] * sections
    totals = [None] * sections
    part_shapes = [((tiles // 2, chunk, ch), f32), ((tiles // 2, chunk, ch), bf16)]
    whole = pltpu.VMEM((taps, ch), f32)
    for section in range(sections - 1, 0, -1):
        x, pre, p1, p2, pieces, count = kept[section]
        _, below, _, _, below_pieces, below_count = kept[section - 1]
        last = section == sections - 1
        stack, grad, grad_u, near, sums, totals[section] = call(
            functools.partial(back_kernel, section, count, below_count, last, n),
            [
                (stack_shape, bf16),
                (tile_shape, bf16),
                (tile_shape, f32),
                (near_shape, bf16),
                (sum_shape, f32),
                (sum_shape, f32),
            ],
            (
                *pieces,
                *grads,
                *below_pieces,
                below,
                slopes[section - 1],
                grad_u,
                grad,
                g1,
                g2,
                pre,
                p1,
                p2,
                slopes[section],
                gbs,
                weights,
            ),
            [blocks],
            flops=flops,
            name="backward",
        )
        g1, g2, grads, total = exchange(sums, near, grad)
        parts[section] = call(
            weight_kernel,
            part_shapes,
            (x, after(stack, total)),
            [whole],
            flops=flops,
            name="weight",
        )
        grads[0] = after(grads[0], parts[section][1])
    x, pre, p1, p2, pieces, count = kept[0]
    last = sections == 1
    stack, *parts[0], totals[0] = call(
        functools.partial(final_weight_kernel, 0, count, last, n),
        [(stack_shape, bf16), *part_shapes, (sum_shape, f32)],
        (*pieces, *grads, grad_u, g1, pre, p1, slopes[0], gbs, x),
        [whole],
        flops=flops,
        name="weight",
    )

    def finish(signal):
        (feature_grad,) = call(
            functools.partial(final_grad_kernel, 0, count, last, n),
            [((1,) + tile_shape, bf16)],
            (*pieces, *grads, grad, g2, pre, p2, gbs, weights, after(stack, signal)),
            [outer, blocks],
            flops=flops,
            name="final_grad",
        )
        last_x, last_pre, _, _, last_pieces, last_count = kept[-1]
        (neck,) = call(
            functools.partial(neck_kernel, last_count, n, sections - 1),
            [((1,) + tile_shape, bf16)],
            (last_x, after(last_pre, signal), *last_pieces, gbs),
            flops=flops,
            name="neck",
        )
        return neck, feature_grad

    m = sections
    if direct:
        size = taps // 2
        theirs = [swap(p[1], "row", 1) for p in parts]
        own, *sending = call(
            functools.partial(chip_kernel, m),
            [((size + 8, ch), f32)] + [((size + 32, ch), bf16)] * 3,
            (*[p[0] for p in parts], *theirs, *totals),
            [pltpu.VMEM((m, size, ch), f32), pltpu.VMEM((m, 8, ch), f32)],
            name="chips",
        )
        received = [swap(v, "section", d + 1) for d, v in enumerate(sending)]
        neck, feature_grad = finish(own)
        received[0] = after(received[0], (neck, feature_grad))
        mine, one, two, three, total = call(
            section_kernel,
            [((chunk, ch), f32)] + [((chunk, ch), bf16)] * 3 + [(sum_shape, f32)],
            (own, *received),
            [pltpu.VMEM((tiles // 2, chunk, ch), f32)],
            name="sections",
        )
        chunks = [swap(v, "row", 2 * (k + 1)) for k, v in enumerate((one, two, three))]
        weight_grad, gain_grad, bias_grad = call(
            last_kernel,
            [((1, chunk, ch), f32), ((1, ch), f32), ((1, ch), f32)],
            (mine, *chunks, total),
            name="last",
        )
    else:
        lanes = [list(range(c, tiles, 2)) for c in range(2)]
        here = lax.axis_index("section")
        chip_sums = jnp.stack([p[0] + swap(p[1], "row", 1).astype(f32) for p in parts])
        sums = jnp.stack(totals)

        def over_sections(stacked):
            total, *others = [
                lax.dynamic_index_in_dim(stacked, here ^ d, 0, keepdims=False) for d in range(4)
            ]
            for d, other in enumerate(others):
                total = total + swap(other, "section", d + 1)
            return total

        chip_sum, total = over_sections(chip_sums), over_sections(sums)
        weight_grad = lax.psum_scatter(
            chip_sum, "row", scatter_dimension=0, tiled=True, axis_index_groups=lanes
        )
        gain_grad, bias_grad = total[0:1], total[1:2]
        neck, feature_grad = finish(total)
    return neck, feature_grad, weight_grad, gain_grad, bias_grad


def solution(mesh):
    return jax.shard_map(
        per_device,
        mesh=mesh,
        in_specs=(
            P("section", None, "row", None, None),
            P("section", None, None),
            P("section", None),
            P("section", None),
            P(None, None, "row", None),
            P("section", None, "row", None, None),
        ),
        out_specs=(
            P("section", None, "row", None, None),
            P("section", None, "row", None, None),
            P("section", "row", None),
            P("section", None),
            P("section", None),
        ),
        check_vma=False,
    )
```

```python
import functools

import jax
import jax.numpy as jnp
from jax import lax
from jax.experimental import pallas as pl
from jax.experimental.pallas import tpu as pltpu
from jax.sharding import PartitionSpec as P

norm_eps = 1e-05
hole = -1e30
hole_edge = -1e29
f32 = jnp.float32
bf16 = jnp.bfloat16
VMEM_SPEC = pl.BlockSpec(memory_space=pltpu.VMEM)


class Place:
    def __init__(self):
        tile = lax.axis_index("row")
        self.section = lax.axis_index("section")
        self.core = lax.rem(tile, 2)
        self.even = self.core == 0
        self.chip = tile // 2
        outer = jnp.where(self.even, 0, lax.axis_size("row") - 1)
        self.inside = (tile != outer).astype(f32)

    def row(self, q, rows):
        return jnp.where(self.even, rows - 1 - q, q)

    def tap(self, i):
        return jnp.where(self.even, 2 - i, i)


def shifted(value, step):
    cols = value.shape[0]
    index = lax.broadcasted_iota(jnp.int32, value.shape, 0)
    edge = 0 if step == 1 else cols - 1
    return jnp.where(index == edge, 0.0, pltpu.roll(value, step % cols, 0))


def shifts(value, flip):
    left, right = shifted(value, 1).astype(bf16), shifted(value, -1).astype(bf16)
    return (right, value.astype(bf16), left) if flip else (left, value.astype(bf16), right)


def put_row(stack, scene, k, value, flip):
    ch = value.shape[1]
    for j, part in enumerate(shifts(value, flip)):
        stack[j, k // 2, scene, :, (k % 2) * ch : (k % 2 + 1) * ch] = part


def put_outer(outer, scene, value, flip):
    for j, part in enumerate(shifts(value, flip)):
        outer[j, scene] = part


def put_blocks(kernel_rows, blocks):
    ch = kernel_rows.shape[1]

    def tap(i, j):
        return kernel_rows[(3 * i + j) * ch : (3 * i + j + 1) * ch, :]

    zero = jnp.zeros((ch, ch), bf16)
    for j in range(3):
        blocks[2 * j, :ch, :ch] = tap(0, j)
        blocks[2 * j, :ch, ch:] = zero
        blocks[2 * j, ch:, :ch] = tap(1, j)
        blocks[2 * j, ch:, ch:] = tap(0, j)
        blocks[2 * j + 1, :ch, :ch] = tap(2, j)
        blocks[2 * j + 1, :ch, ch:] = tap(1, j)
        blocks[2 * j + 1, ch:, :ch] = zero
        blocks[2 * j + 1, ch:, ch:] = tap(2, j)


def operand(stack, outer, scene, j, pair):
    if outer is None or pair + 1 < stack.shape[1]:
        return stack[j, pair, scene]
    ch = outer.shape[-1]
    return jnp.concatenate([stack[j, pair, scene, :, :ch], outer[j, scene]], axis=1)


def conv_pair(stack, outer, blocks, scene, p):
    lhs = [operand(stack, outer, scene, j, p + h) for j in range(3) for h in range(2)]
    rhs = jnp.concatenate([blocks[n] for n in range(6)], axis=0)
    return jnp.dot(jnp.concatenate(lhs, axis=1), rhs, preferred_element_type=f32)


def conv_back_pair(stack, outer, blocks, scene, p):
    total = None
    for j in range(3):
        for h in range(2):
            term = lax.dot_general(
                operand(stack, outer, scene, j, p + h),
                blocks[2 * j + 1 - h],
                (((1,), (1,)), ((), ())),
                preferred_element_type=f32,
            )
            total = term if total is None else total + term
    return total


def summed(pieces):
    total = pieces[0][...]
    for piece in pieces[1:]:
        total = total + piece[...]
    return total


def norm_stats(total, count):
    count = total[2:3] if count is None else count
    mean = total[0:1] / count
    inv = lax.rsqrt(total[1:2] / count - mean * mean + norm_eps)
    return mean, inv, count


def half_affine(mean, inv, gb):
    scale = inv * gb[0:1]
    return 0.5 * scale, 0.5 * (gb[1:2] - mean * scale)


def twice_slope(half, t):
    return (1.0 + t) + half * (1.0 - t * t)


def fold(value):
    return jnp.sum(value.reshape(-1, 8, value.shape[-1]), axis=0)


def plus(total, term):
    return term if total is None else total + term


def sum_rows(first, second, third=None):
    ch = first.shape[1]
    rows = [jnp.sum(first, axis=0, keepdims=True), jnp.sum(second, axis=0, keepdims=True)]
    rows.append(jnp.zeros((1, ch), f32) if third is None else third)
    return jnp.concatenate(rows + [jnp.zeros((5, ch), f32)], axis=0)


def put_parts(out, start, total):
    hi = total.astype(bf16).astype(f32)
    left = total - hi
    mid = left.astype(bf16).astype(f32)
    parts = [hi, mid, left - mid, jnp.zeros_like(total)]
    out[start : start + 16, :] = jnp.concatenate(parts[:2], axis=0).astype(bf16)
    out[start + 16 : start + 32, :] = jnp.concatenate(parts[2:], axis=0).astype(bf16)


def put_sums(sums, near, total):
    sums[...] = total
    if near is not None:
        put_parts(near, near.shape[0] - 32, total)


def mask_columns(rows):
    count, cols = rows.shape
    filled = jnp.concatenate([rows, jnp.zeros((128 - count, cols), f32)], axis=0)
    return filled.T


def mask_rows(place, mask):
    scenes, rows = mask.shape[1:3]
    parts = []
    for s in range(scenes):
        parts += [mask[place.section, s, pl.ds(place.row(q, rows), 1), :].astype(f32) for q in range(rows)]
    return jnp.concatenate(parts, axis=0)


def prep_kernel(mask, features, cot, weight, gain, bias, near, far, out, held, rows_mask, both, sems):
    place = Place()
    scenes, rows, cols, ch = features.shape[1:]
    half = weight.shape[1] // 2
    mine = pl.ds(pl.multiple_of(place.core * half, 16), half)
    moves = [
        (weight.at[0, mine], out.at[pl.ds(0, half)]),
        (gain, both.at[pl.ds(0, 1)]),
        (bias, both.at[pl.ds(1, 1)]),
        (mask.at[pl.ds(place.section, 1)], rows_mask),
    ]
    for source in (features, cot):
        for q in (0, rows - 1):
            moves.append((source.at[0, :, place.row(q, rows)], held.at[len(moves) - 4]))
    copies = [pltpu.make_async_copy(a, b, sems.at[n]) for n, (a, b) in enumerate(moves)]
    for copy in copies:
        copy.start()
    both[2:8] = jnp.zeros((6, ch), f32)
    for copy in copies:
        copy.wait()
    put_parts(out, half, both[...])
    parts = []
    for s in range(scenes):
        for q in (0, rows - 1):
            parts.append(rows_mask[0, s, pl.ds(place.row(q, rows), 1), :].astype(f32))
    columns = mask_columns(jnp.concatenate(parts, axis=0))
    size = scenes * cols
    for s in range(scenes):
        here = slice(s * cols, (s + 1) * cols)
        there = slice(size + s * cols, size + (s + 1) * cols)
        for n, edge in enumerate((near, far)):
            at = 2 * s + n
            edge[here, :] = (held[n, s].astype(f32) * columns[:, at : at + 1]).astype(bf16)
            edge[there, :] = held[2 + n, s]


def gather_kernel(own, gain, bias, r1, r2, r3, other, weights, gbs):
    place = Place()
    taps, ch = own.shape[1:]
    piece = taps // 6

    def put(section, p, rows):
        at = (2 * place.tap(p // 2) + p % 2) * piece
        weights[section, pl.ds(pl.multiple_of(at, 16), piece), :] = rows

    for p in range(6):
        put(place.section, p, own[0, p * piece : (p + 1) * piece])
    gbs[place.section] = jnp.concatenate([gain[...], bias[...], jnp.zeros((6, ch), f32)], axis=0)
    for d, got in ((1, r1), (2, r2), (3, r3)):
        there = place.section ^ d
        for n in range(3):
            rows = slice(n * piece, (n + 1) * piece)
            put(there, 3 * place.core + n, got[rows])
            put(there, 3 * (1 - place.core) + n, other[d - 1, rows])
        parts = got[3 * piece :].astype(f32)
        gbs[there] = parts[0:8] + parts[8:16] + parts[16:24]


def far_kernel(rows_ref, far):
    scenes, rows, cols, ch = rows_ref.shape
    for s in range(scenes):
        far[s * cols : (s + 1) * cols, :] = rows_ref[s, rows - 1].astype(bf16)


def finish_forward(stack, blocks, pre, near, sums, make_rows, columns, third):
    scenes, rows, cols, ch = pre.shape
    first = second = None
    make_rows(0)
    for scene in range(scenes):
        if scene + 1 < scenes:
            make_rows(scene + 1)
        for p in range(rows // 2):
            both = conv_pair(stack, None, blocks, scene, p)
            for n in range(2):
                r = 2 * p + n
                kept = row = both[:, n * ch : (n + 1) * ch]
                if columns is not None:
                    at = scene * rows + r
                    inside = columns[:, at : at + 1] > 0.5
                    kept = jnp.where(inside, row, hole)
                    row = jnp.where(inside, row, 0.0)
                pre[scene, r] = kept
                if r == 0:
                    near[scene * cols : (scene + 1) * cols, :] = kept.astype(bf16)
                first = plus(first, fold(row))
                second = plus(second, fold(row * row))
    put_sums(sums, near, sum_rows(first, second, third))


def first_kernel(mask, features, near, far, weights, x, pre, near_out, sums, stack, blocks):
    scenes, rows, cols, ch = features.shape[1:]
    put_blocks(weights.at[0], blocks)
    place = Place()
    mask_now = mask_rows(place, mask)
    columns = mask_columns(mask_now)

    def make_rows(scene):
        here = slice(scene * cols, (scene + 1) * cols)
        for k in range(rows + 2):
            if k == 0:
                value = near[here, :].astype(f32)
            elif k == rows + 1:
                value = far[here, :].astype(f32)
            else:
                at = scene * rows + k - 1
                value = features[0, scene, place.row(k - 1, rows)].astype(f32) * columns[:, at : at + 1]
            x[scene, k] = value.astype(bf16)
            put_row(stack, scene, k, value, False)

    total = jnp.sum(jnp.sum(mask_now, axis=1, keepdims=True), axis=0, keepdims=True)
    third = jnp.broadcast_to(total, (1, ch))
    finish_forward(stack, blocks, pre, near_out, sums, make_rows, columns, third)


def next_kernel(section, count, n, x_in, pre_in, near, far, *rest):
    pieces, rest = rest[:n], rest[n:]
    gbs, weights, x, pre, near_out, sums, stack, blocks = rest
    scenes, rows, cols, ch = pre.shape
    put_blocks(weights.at[section], blocks)
    scale, offset = stat_affine(pieces, count, gbs[section - 1])
    inside = Place().inside

    def make_rows(scene):
        here = slice(scene * cols, (scene + 1) * cols)
        for k in range(rows + 2):
            if k == 0:
                act = act_of(near[here, :].astype(f32), scale, offset, count)
            elif k == rows + 1:
                act = inside * act_of(far[here, :].astype(f32), scale, offset, count)
            else:
                act = act_of(pre_in[scene, k - 1], scale, offset, count)
            value = x_in[scene, k].astype(f32) + act
            x[scene, k] = value.astype(bf16)
            put_row(stack, scene, k, value, False)

    finish_forward(stack, blocks, pre, near_out, sums, make_rows, None, None)


def stat_affine(pieces, count, gb):
    mean, inv, _ = norm_stats(summed(pieces), count)
    return half_affine(mean, inv, gb)


def act_of(value, scale, offset, count):
    half = value * scale + offset
    act = half * jnp.tanh(half) + half
    return jnp.where(value > hole_edge, act, 0.0) if count is None else act


def slope_of(value, scale, offset, count):
    half = value * scale + offset
    out = twice_slope(half, jnp.tanh(half))
    return jnp.where(value > hole_edge, out, 0.0) if count is None else out


def at_scene(scene, cols):
    start = scene * cols
    return pl.ds(start if isinstance(scene, int) else pl.multiple_of(start, 16), cols)


def slope_kernel(section, count, n, pre, near, *rest):
    pieces, (gbs, slope) = rest[:n], rest[n:]
    scenes, padded, cols, ch = slope.shape
    scale, offset = stat_affine(pieces, count, gbs[section])

    @pl.loop(0, scenes)
    def _(scene):
        for k in range(padded):
            value = pre[scene, k - 1] if k else near[at_scene(scene, cols), :].astype(f32)
            slope[scene, k] = slope_of(value, scale, offset, count)


def turn_kernel(count, n, section, pre, cot, *rest):
    pieces, (gbs, grad_u, sums) = rest[:n], rest[n:]
    scenes, rows, cols, ch = grad_u.shape
    mean, inv, _ = norm_stats(summed(pieces), count)
    scale, offset = half_affine(mean, inv, gbs[section])
    place = Place()

    def one(scene, total):
        first, second = total
        for q in range(rows):
            value = pre[scene, q]
            grad = cot[0, scene, place.row(q, rows)].astype(f32) * slope_of(value, scale, offset, count)
            grad_u[scene, q] = grad
            first = first + fold(grad * value)
            second = second + fold(grad)
        return first, second

    zero = jnp.zeros((8, ch), f32)
    first, second = lax.fori_loop(0, scenes, one, (zero, zero))
    put_sums(sums, None, grad_sums(first, second, mean, inv))


def grad_sums(by_pre, plain, mean, inv):
    by_pre = 0.5 * jnp.sum(by_pre, axis=0, keepdims=True)
    plain = 0.5 * jnp.sum(plain, axis=0, keepdims=True)
    return jnp.concatenate(
        [inv * (by_pre - mean * plain), plain, jnp.zeros((6, plain.shape[1]), f32)], axis=0
    )


def neck_kernel(count, n, section, x, pre, *rest):
    pieces, (gbs, neck) = rest[:n], rest[n:]
    scenes, rows = neck.shape[1:3]
    scale, offset = stat_affine(pieces, count, gbs[section])
    place = Place()

    @pl.loop(0, scenes)
    def _(scene):
        for q in range(rows):
            act = act_of(pre[scene, q], scale, offset, count)
            neck[0, scene, place.row(q, rows)] = (x[scene, q + 1].astype(f32) + act).astype(bf16)


def back_terms(section, count, pieces, grads, gbs):
    mean, inv, cells = norm_stats(summed(pieces), count)
    total = summed(grads)
    lead = inv * gbs[section][0:1]
    by_pre = -lead * inv * total[0:1] / cells
    constant = -lead * total[1:2] / cells - by_pre * mean
    return (0.5 * lead, by_pre, constant), total


def grad_pre(terms, lifted, value, count):
    lead, by_pre, constant = terms
    out = lead * lifted + (by_pre * value + constant)
    return jnp.where(value > hole_edge, out, 0.0) if count is None else out


def back_rows(count, last, terms, stack, grad_u, g1, pre, p1, slope):
    scenes, rows, cols, ch = grad_u.shape
    base = scenes * cols if last else 0

    def make_rows(scene):
        at = scene * cols
        for k in range(rows + 1):
            if k:
                value = pre[scene, k - 1]
                lifted = grad_u[scene, k - 1]
            else:
                value = p1[at : at + cols, :].astype(f32)
                lifted = g1[base + at : base + at + cols, :].astype(f32) * slope[scene, 0]
            put_row(stack, scene, k, grad_pre(terms, lifted, value, count), True)

    return make_rows


def back_outer_row(section, count, last, terms, g2, p2, pieces, gbs, cols):
    base = p2.shape[0] if last else 0
    scale, offset = stat_affine(pieces, count, gbs[section])
    inside = Place().inside

    def outer_row(scene):
        at = at_scene(scene, cols)
        value = p2[at, :].astype(f32)
        lifted = g2[pl.ds(base + at.start, cols), :].astype(f32) * slope_of(value, scale, offset, count)
        return inside * grad_pre(terms, lifted, value, count)

    return outer_row


def grad_row(grad_in, last, scene, q, rows):
    return grad_in[0, scene, Place().row(q, rows)] if last else grad_in[scene, q]


def back_kernel(section, count, count_below, last, n, *rest):
    pieces, rest = rest[:n], rest[n:]
    grads, rest = rest[:n], rest[n:]
    pieces_below, rest = rest[:n], rest[n:]
    pre_below, slope_below, grad_u, grad_in, g1, g2, pre, p1, p2, slope, gbs, weights, *rest = rest
    stack, grad_out, grad_u_below, near, sums, total_out, blocks = rest
    scenes, rows, cols, ch = grad_u.shape
    put_blocks(weights.at[section], blocks)
    terms, total = back_terms(section, count, pieces, grads, gbs)
    total_out[...] = total
    mean_below, inv_below, _ = norm_stats(summed(pieces_below), count_below)
    make_rows = back_rows(count, last, terms, stack, grad_u, g1, pre, p1, slope)
    outer_row = back_outer_row(section, count, last, terms, g2, p2, pieces, gbs, cols)

    def make_all(scene):
        make_rows(scene)
        put_row(stack, scene, rows + 1, outer_row(scene), True)

    first = second = None
    make_all(0)
    for scene in range(scenes):
        if scene + 1 < scenes:
            make_all(scene + 1)
        for p in range(rows // 2):
            both = conv_back_pair(stack, None, blocks, scene, p)
            for m in range(2):
                r = 2 * p + m
                grad = grad_row(grad_in, last, scene, r, rows).astype(f32)
                grad = (grad + both[:, m * ch : (m + 1) * ch]).astype(bf16)
                grad_out[scene, r] = grad
                if r == 0:
                    near[scene * cols : (scene + 1) * cols, :] = grad
                lifted = grad.astype(f32) * slope_below[scene, r + 1]
                grad_u_below[scene, r] = lifted
                first = plus(first, fold(lifted * pre_below[scene, r]))
                second = plus(second, fold(lifted))
    put_sums(sums, near, grad_sums(first, second, mean_below, inv_below))


def final_weight_kernel(section, count, last, n, *rest):
    pieces, rest = rest[:n], rest[n:]
    grads, rest = rest[:n], rest[n:]
    grad_u, g1, pre, p1, slope, gbs, x, stack, mine, theirs, total_out, whole = rest
    terms, total = back_terms(section, count, pieces, grads, gbs)
    total_out[...] = total
    make_rows = back_rows(count, last, terms, stack, grad_u, g1, pre, p1, slope)
    weight_body(x, stack, mine, theirs, whole, make_rows)


def final_grad_kernel(section, count, last, n, *rest):
    pieces, rest = rest[:n], rest[n:]
    grads, rest = rest[:n], rest[n:]
    grad_in, g2, pre, p2, gbs, weights, stack, grad_out, outer, blocks = rest
    scenes, rows, cols, ch = grad_out.shape[1:]
    put_blocks(weights.at[section], blocks)
    terms, _ = back_terms(section, count, pieces, grads, gbs)
    outer_row = back_outer_row(section, count, last, terms, g2, p2, pieces, gbs, cols)
    place = Place()

    @pl.loop(0, scenes)
    def _(scene):
        put_outer(outer, scene, outer_row(scene), True)
        for p in range(rows // 2):
            both = conv_back_pair(stack, outer, blocks, scene, p)
            for m in range(2):
                r = 2 * p + m
                grad = grad_row(grad_in, last, scene, r, rows).astype(f32)
                grad = grad + both[:, m * ch : (m + 1) * ch]
                if count is None:
                    grad = jnp.where(pre[scene, r] > hole_edge, grad, 0.0)
                grad_out[0, scene, place.row(r, rows)] = grad.astype(bf16)


def weight_kernel(x, stack, mine, theirs, whole):
    weight_body(x, stack, mine, theirs, whole, None)


def weight_body(x, stack, mine, theirs, whole, make_rows):
    scenes, padded, cols, ch = x.shape
    rows = padded - 2
    place = Place()
    total = None
    if make_rows:
        make_rows(0)
    for scene in range(scenes):
        if make_rows and scene + 1 < scenes:
            make_rows(scene + 1)
        lines = [x[scene, k] for k in range(rows + 2)]
        lhs = jnp.concatenate(
            [jnp.concatenate(lines[i : i + rows], axis=0) for i in range(3)], axis=1
        )
        rhs = jnp.concatenate(
            [
                jnp.concatenate(
                    [
                        stack[j, k // 2, scene, :, (k % 2) * ch : (k % 2 + 1) * ch]
                        for j in range(3)
                    ],
                    axis=1,
                )
                for k in range(1, rows + 1)
            ],
            axis=0,
        )
        term = lax.dot_general(lhs, rhs, (((0,), (0,)), ((), ())), preferred_element_type=f32)
        total = plus(total, term)
    for i in range(3):
        for j in range(3):
            at = pl.multiple_of((3 * place.tap(i) + j) * ch, 8)
            whole[pl.ds(at, ch), :] = total[i * ch : (i + 1) * ch, j * ch : (j + 1) * ch]
    chips, chunk = mine.shape[:2]
    for z in range(chips):
        at = pl.multiple_of((2 * z + place.core) * chunk, 8)
        mine[z] = whole[pl.ds(at, chunk), :]
        at = pl.multiple_of((2 * z + 1 - place.core) * chunk, 8)
        theirs[z] = whole[pl.ds(at, chunk), :].astype(bf16)


def chip_kernel(n, *refs):
    mine, refs = refs[:n], refs[n:]
    theirs, refs = refs[:n], refs[n:]
    totals, refs = refs[:n], refs[n:]
    outs, held, sums = refs[:4], refs[4], refs[5]
    here = Place().section
    chips, chunk, ch = mine[0].shape
    for s in range(n):
        for z in range(chips):
            held[s, z * chunk : (z + 1) * chunk] = mine[s][z] + theirs[s][z].astype(f32)
        sums[s] = totals[s][...]
    size = chips * chunk
    for d in range(4):
        if d:
            outs[d][:size] = held[here ^ d].astype(bf16)
            put_parts(outs[d], size, sums[here ^ d])
        else:
            outs[0][:size] = held[here]
            outs[0][size:] = sums[here]


def section_kernel(own, a, b, c, mine, one, two, three, sums, held):
    chips, chunk = held.shape[:2]
    size = chips * chunk
    for z in range(chips):
        at = slice(z * chunk, (z + 1) * chunk)
        held[z] = own[at] + a[at].astype(f32) + b[at].astype(f32) + c[at].astype(f32)
    total = own[size:]
    for got in (a, b, c):
        parts = got[size:].astype(f32)
        total = total + (parts[0:8] + parts[8:16] + parts[16:24])
    sums[...] = total
    chip = Place().chip
    mine[...] = held[chip]
    for k, out in ((1, one), (2, two), (3, three)):
        out[...] = held[chip ^ k].astype(bf16)


def last_kernel(mine, a, b, c, sums, weight, gain, bias):
    gain[...] = sums[0:1]
    bias[...] = sums[1:2]
    weight[0] = mine[...] + a[...].astype(f32) + b[...].astype(f32) + c[...].astype(f32)


def call(body, outs, ins, scratch=(), flops=0, name=None, hbm=()):
    specs = [VMEM_SPEC] * len(ins)
    for n in hbm:
        specs[n] = pl.BlockSpec(memory_space=pltpu.HBM)
    return pl.pallas_call(
        body,
        out_shape=[jax.ShapeDtypeStruct(s, d) for s, d in outs],
        in_specs=specs,
        out_specs=[VMEM_SPEC] * len(outs),
        scratch_shapes=list(scratch),
        compiler_params=pltpu.CompilerParams(vmem_limit_bytes=12 * 2**20),
        cost_estimate=pl.CostEstimate(flops=flops, bytes_accessed=0, transcendentals=0),
        name=name,
    )(*ins)


def swap(value, axis, step):
    count = lax.axis_size(axis)
    return lax.ppermute(value, axis, [(i, i ^ step) for i in range(count)])


def swap_next(value):
    pairs = []
    for i in range(1, lax.axis_size("row") - 1, 2):
        pairs += [(i, i + 1), (i + 1, i)]
    return lax.ppermute(value, "row", pairs)


def row_pieces(total):
    count = lax.axis_size("row")
    stride = 2
    while True:
        group = min(4, count // stride)
        pieces = [total] + [swap(total, "row", k * stride + (stride == 2)) for k in range(1, group)]
        stride *= group
        if stride >= count:
            return pieces
        total = sum(pieces[1:], pieces[0])


def after(value, signal):
    return lax.optimization_barrier((value, signal))[0]


def far_rows(rows_ref):
    scenes, _, cols, ch = rows_ref.shape
    (far,) = call(far_kernel, [((scenes * cols, ch), bf16)], (rows_ref,), name="far")
    return far


def exchange(sums, near, rows_ref=None):
    got = swap(near, "row", 1)
    far = None if rows_ref is None else swap_next(far_rows(rows_ref))
    parts = got[got.shape[0] - 32 :].astype(f32)
    total = sums + (parts[0:8] + parts[8:16] + parts[16:24])
    return got, far, row_pieces(total), total


def per_device(features, conv_weight, norm_gain, norm_bias, valid_mask, out_cotangent):
    sections = lax.axis_size("section")
    tiles = lax.axis_size("row")
    scenes, rows, cols, ch = features.shape[1:]
    taps = conv_weight.shape[1]
    cells = float(scenes * rows * cols * tiles)
    tile_shape = (scenes, rows, cols, ch)
    pad_shape = (scenes, rows + 2, cols, ch)
    slope_shape = (scenes, rows + 1, cols, ch)
    edge = scenes * cols
    near_shape = (edge + 32, ch)
    sum_shape = (8, ch)
    stack_shape = (3, rows // 2 + 1, scenes, cols, 2 * ch)
    blocks = pltpu.VMEM((6, 2 * ch, 2 * ch), bf16)
    outer = pltpu.VMEM((3, scenes, cols, ch), bf16)
    flops = 2 * scenes * rows * cols * taps * ch
    half = taps // 2
    chunk = taps // tiles
    direct = tiles == 8 and chunk % 16 == 0

    def in_hbm(*values):
        return [pltpu.with_memory_space_constraint(v, pltpu.HBM) for v in values]

    e1, e2, wsend = call(
        prep_kernel,
        [((2 * edge, ch), bf16), ((2 * edge, ch), bf16), ((half + 32, ch), bf16)],
        in_hbm(valid_mask, features, out_cotangent, conv_weight, norm_gain, norm_bias),
        [
            pltpu.VMEM((4, scenes, cols, ch), bf16),
            pltpu.VMEM((1, scenes, rows, cols), jnp.int32),
            pltpu.VMEM((8, ch), f32),
            pltpu.SemaphoreType.DMA((8,)),
        ],
        hbm=range(6),
        name="prep",
    )
    got = [swap(wsend, "section", d) for d in (1, 2, 3)]
    e1 = swap(e1, "row", 1)
    e2 = swap_next(e2)
    got[1] = after(got[1], e1)
    other = swap(jnp.stack(got), "row", 1)
    weights, gbs = call(
        gather_kernel,
        [((sections, taps, ch), bf16), ((sections, 8, ch), f32)],
        (conv_weight, norm_gain, norm_bias, *got, other),
        name="gather",
    )

    forward_outs = [(pad_shape, bf16), (tile_shape, f32), (near_shape, bf16), (sum_shape, f32)]
    scratch = [pltpu.VMEM(stack_shape, bf16), blocks]
    kept = []
    slopes = []
    x, pre, near, sums = call(
        first_kernel,
        forward_outs,
        (valid_mask, features, e1, e2, weights),
        scratch,
        flops=flops,
        name="forward",
    )
    for section in range(sections):
        count = None if section == 0 else cells
        near, far, pieces, total = exchange(sums, near, pre)
        if section > 0:
            _, below, below_near, _, below_pieces, below_count = kept[-1]
            slopes += call(
                functools.partial(slope_kernel, section - 1, below_count, len(pieces)),
                [(slope_shape, f32)],
                (after(below, total), below_near, *below_pieces, gbs),
                name="slope",
            )
            pieces[0] = after(pieces[0], slopes[-1])
        kept.append((x, pre, near, far, pieces, count))
        if section == sections - 1:
            break
        x, pre, near, sums = call(
            functools.partial(next_kernel, section + 1, count, len(pieces)),
            forward_outs,
            (x, pre, near, far, *pieces, gbs, weights),
            scratch,
            flops=flops,
            name="forward",
        )
    n = len(pieces)
    grad_u, sums = call(
        functools.partial(turn_kernel, count, n, sections - 1),
        [(tile_shape, f32), (sum_shape, f32)],
        (pre, out_cotangent, *pieces, gbs),
        name="turn",
    )
    total = sums + swap(sums, "row", 1)
    grads = row_pieces(total)
    slopes += call(
        functools.partial(slope_kernel, sections - 1, count, n),
        [(slope_shape, f32)],
        (after(pre, total), near, *pieces, gbs),
        name="slope",
    )
    grad, g1, g2 = out_cotangent, e1, e2
    parts = [None] * sections
    totals = [None] * sections
    part_shapes = [((tiles // 2, chunk, ch), f32), ((tiles // 2, chunk, ch), bf16)]
    whole = pltpu.VMEM((taps, ch), f32)
    for section in range(sections - 1, 0, -1):
        x, pre, p1, p2, pieces, count = kept[section]
        _, below, _, _, below_pieces, below_count = kept[section - 1]
        last = section == sections - 1
        stack, grad, grad_u, near, sums, totals[section] = call(
            functools.partial(back_kernel, section, count, below_count, last, n),
            [
                (stack_shape, bf16),
                (tile_shape, bf16),
                (tile_shape, f32),
                (near_shape, bf16),
                (sum_shape, f32),
                (sum_shape, f32),
            ],
            (
                *pieces,
                *grads,
                *below_pieces,
                below,
                slopes[section - 1],
                grad_u,
                grad,
                g1,
                g2,
                pre,
                p1,
                p2,
                slopes[section],
                gbs,
                weights,
            ),
            [blocks],
            flops=flops,
            name="backward",
        )
        g1, g2, grads, total = exchange(sums, near, grad if section > 1 else None)
        parts[section] = call(
            weight_kernel,
            part_shapes,
            (x, after(stack, total)),
            [whole],
            flops=flops,
            name="weight",
        )
        grads[0] = after(grads[0], parts[section][1])
    x, pre, p1, p2, pieces, count = kept[0]
    last = sections == 1
    stack, *parts[0], totals[0] = call(
        functools.partial(final_weight_kernel, 0, count, last, n),
        [(stack_shape, bf16), *part_shapes, (sum_shape, f32)],
        (*pieces, *grads, grad_u, g1, pre, p1, slopes[0], gbs, x),
        [whole],
        flops=flops,
        name="weight",
    )

    def finish_neck(signal):
        far = swap_next(far_rows(after(grad, signal)))
        last_x, last_pre, _, _, last_pieces, last_count = kept[-1]
        (neck,) = call(
            functools.partial(neck_kernel, last_count, n, sections - 1),
            [((1,) + tile_shape, bf16)],
            (last_x, after(last_pre, signal), *last_pieces, gbs),
            flops=8 * flops,
            name="neck",
        )
        return neck, far

    def finish_grad(far, signal):
        (feature_grad,) = call(
            functools.partial(final_grad_kernel, 0, count, last, n),
            [((1,) + tile_shape, bf16)],
            (*pieces, *grads, grad, far, pre, p2, gbs, weights, after(stack, signal)),
            [outer, blocks],
            flops=flops,
            name="final_grad",
        )
        return feature_grad

    m = sections
    if direct:
        size = taps // 2
        theirs = [swap(p[1], "row", 1) for p in parts]
        own, *sending = call(
            functools.partial(chip_kernel, m),
            [((size + 8, ch), f32)] + [((size + 32, ch), bf16)] * 3,
            (*[p[0] for p in parts], *theirs, *totals),
            [pltpu.VMEM((m, size, ch), f32), pltpu.VMEM((m, 8, ch), f32)],
            name="chips",
        )
        received = [swap(v, "section", d + 1) for d, v in enumerate(sending)]
        neck, far = finish_neck(own)
        received[0] = after(received[0], neck)
        mine, one, two, three, total = call(
            section_kernel,
            [((chunk, ch), f32)] + [((chunk, ch), bf16)] * 3 + [(sum_shape, f32)],
            (own, *received),
            [pltpu.VMEM((tiles // 2, chunk, ch), f32)],
            name="sections",
        )
        chunks = [swap(v, "row", 2 * (k + 1)) for k, v in enumerate((one, two, three))]
        feature_grad = finish_grad(far, total)
        mine = after(mine, feature_grad)
        weight_grad, gain_grad, bias_grad = call(
            last_kernel,
            [((1, chunk, ch), f32), ((1, ch), f32), ((1, ch), f32)],
            (mine, *chunks, total),
            name="last",
        )
    else:
        lanes = [list(range(c, tiles, 2)) for c in range(2)]
        here = lax.axis_index("section")
        chip_sums = jnp.stack([p[0] + swap(p[1], "row", 1).astype(f32) for p in parts])
        sums = jnp.stack(totals)

        def over_sections(stacked):
            total, *others = [
                lax.dynamic_index_in_dim(stacked, here ^ d, 0, keepdims=False) for d in range(4)
            ]
            for d, other in enumerate(others):
                total = total + swap(other, "section", d + 1)
            return total

        chip_sum, total = over_sections(chip_sums), over_sections(sums)
        weight_grad = lax.psum_scatter(
            chip_sum, "row", scatter_dimension=0, tiled=True, axis_index_groups=lanes
        )
        gain_grad, bias_grad = total[0:1], total[1:2]
        neck, far = finish_neck(total)
        feature_grad = finish_grad(far, neck)
    return neck, feature_grad, weight_grad, gain_grad, bias_grad


def solution(mesh):
    return jax.shard_map(
        per_device,
        mesh=mesh,
        in_specs=(
            P("section", None, "row", None, None),
            P("section", None, None),
            P("section", None),
            P("section", None),
            P(None, None, "row", None),
            P("section", None, "row", None, None),
        ),
        out_specs=(
            P("section", None, "row", None, None),
            P("section", None, "row", None, None),
            P("section", "row", None),
            P("section", None),
            P("section", None),
        ),
        check_vma=False,
    )
```

```python
import functools

import jax
import jax.numpy as jnp
from jax import lax
from jax.experimental import pallas as pl
from jax.experimental.pallas import tpu as pltpu
from jax.sharding import PartitionSpec as P

norm_eps = 1e-05
hole = -1e30
hole_edge = -1e29
f32 = jnp.float32
bf16 = jnp.bfloat16
VMEM_SPEC = pl.BlockSpec(memory_space=pltpu.VMEM)


class Place:
    def __init__(self):
        tile = lax.axis_index("row")
        self.section = lax.axis_index("section")
        self.core = lax.rem(tile, 2)
        self.even = self.core == 0
        self.chip = tile // 2
        outer = jnp.where(self.even, 0, lax.axis_size("row") - 1)
        self.inside = (tile != outer).astype(f32)

    def row(self, q, rows):
        return jnp.where(self.even, rows - 1 - q, q)

    def tap(self, i):
        return jnp.where(self.even, 2 - i, i)


def shifted(value, step):
    cols = value.shape[0]
    index = lax.broadcasted_iota(jnp.int32, value.shape, 0)
    edge = 0 if step == 1 else cols - 1
    return jnp.where(index == edge, 0.0, pltpu.roll(value, step % cols, 0))


def shifts(value, flip):
    left, right = shifted(value, 1).astype(bf16), shifted(value, -1).astype(bf16)
    return (right, value.astype(bf16), left) if flip else (left, value.astype(bf16), right)


def put_row(stack, scene, k, value, flip):
    ch = value.shape[1]
    for j, part in enumerate(shifts(value, flip)):
        stack[j, k // 2, scene, :, (k % 2) * ch : (k % 2 + 1) * ch] = part


def put_outer(outer, scene, value, flip):
    for j, part in enumerate(shifts(value, flip)):
        outer[j, scene] = part


def put_blocks(kernel_rows, blocks):
    ch = kernel_rows.shape[1]

    def tap(i, j):
        return kernel_rows[(3 * i + j) * ch : (3 * i + j + 1) * ch, :]

    zero = jnp.zeros((ch, ch), bf16)
    for j in range(3):
        blocks[2 * j, :ch, :ch] = tap(0, j)
        blocks[2 * j, :ch, ch:] = zero
        blocks[2 * j, ch:, :ch] = tap(1, j)
        blocks[2 * j, ch:, ch:] = tap(0, j)
        blocks[2 * j + 1, :ch, :ch] = tap(2, j)
        blocks[2 * j + 1, :ch, ch:] = tap(1, j)
        blocks[2 * j + 1, ch:, :ch] = zero
        blocks[2 * j + 1, ch:, ch:] = tap(2, j)


def operand(stack, outer, scene, j, pair):
    if outer is None or pair + 1 < stack.shape[1]:
        return stack[j, pair, scene]
    ch = outer.shape[-1]
    return jnp.concatenate([stack[j, pair, scene, :, :ch], outer[j, scene]], axis=1)


def conv_pair(stack, outer, blocks, scene, p):
    lhs = [operand(stack, outer, scene, j, p + h) for j in range(3) for h in range(2)]
    rhs = jnp.concatenate([blocks[n] for n in range(6)], axis=0)
    return jnp.dot(jnp.concatenate(lhs, axis=1), rhs, preferred_element_type=f32)


def conv_back_pair(stack, outer, blocks, scene, p):
    total = None
    for j in range(3):
        for h in range(2):
            term = lax.dot_general(
                operand(stack, outer, scene, j, p + h),
                blocks[2 * j + 1 - h],
                (((1,), (1,)), ((), ())),
                preferred_element_type=f32,
            )
            total = term if total is None else total + term
    return total


def summed(pieces):
    total = pieces[0][...]
    for piece in pieces[1:]:
        total = total + piece[...]
    return total


def norm_stats(total, count):
    count = total[2:3] if count is None else count
    mean = total[0:1] / count
    inv = lax.rsqrt(total[1:2] / count - mean * mean + norm_eps)
    return mean, inv, count


def half_affine(mean, inv, gb):
    scale = inv * gb[0:1]
    return 0.5 * scale, 0.5 * (gb[1:2] - mean * scale)


def twice_slope(half, t):
    return (1.0 + t) + half * (1.0 - t * t)


def fold(value):
    return jnp.sum(value.reshape(-1, 8, value.shape[-1]), axis=0)


def plus(total, term):
    return term if total is None else total + term


def sum_rows(first, second, third=None):
    ch = first.shape[1]
    rows = [jnp.sum(first, axis=0, keepdims=True), jnp.sum(second, axis=0, keepdims=True)]
    rows.append(jnp.zeros((1, ch), f32) if third is None else third)
    return jnp.concatenate(rows + [jnp.zeros((5, ch), f32)], axis=0)


def put_parts(out, start, total):
    hi = total.astype(bf16).astype(f32)
    left = total - hi
    mid = left.astype(bf16).astype(f32)
    parts = [hi, mid, left - mid, jnp.zeros_like(total)]
    out[start : start + 16, :] = jnp.concatenate(parts[:2], axis=0).astype(bf16)
    out[start + 16 : start + 32, :] = jnp.concatenate(parts[2:], axis=0).astype(bf16)


def put_sums(sums, near, total):
    sums[...] = total
    if near is not None:
        put_parts(near, near.shape[0] - 32, total)


def mask_columns(rows):
    count, cols = rows.shape
    filled = jnp.concatenate([rows, jnp.zeros((128 - count, cols), f32)], axis=0)
    return filled.T


def mask_rows(place, mask):
    scenes, rows = mask.shape[1:3]
    parts = []
    for s in range(scenes):
        parts += [mask[place.section, s, pl.ds(place.row(q, rows), 1), :].astype(f32) for q in range(rows)]
    return jnp.concatenate(parts, axis=0)


def prep_kernel(mask, features, cot, weight, gain, bias, near, far, far_cot, out, held, rows_mask, both, sems):
    place = Place()
    scenes, rows, cols, ch = features.shape[1:]
    half = weight.shape[1] // 2
    mine = pl.ds(pl.multiple_of(place.core * half, 16), half)
    moves = [
        (weight.at[0, mine], out.at[pl.ds(0, half)]),
        (gain, both.at[pl.ds(0, 1)]),
        (bias, both.at[pl.ds(1, 1)]),
        (mask.at[pl.ds(place.section, 1)], rows_mask),
    ]
    for source in (features, cot):
        for q in (0, rows - 1):
            moves.append((source.at[0, :, place.row(q, rows)], held.at[len(moves) - 4]))
    copies = [pltpu.make_async_copy(a, b, sems.at[n]) for n, (a, b) in enumerate(moves)]
    for copy in copies:
        copy.start()
    both[2:8] = jnp.zeros((6, ch), f32)
    for copy in copies:
        copy.wait()
    put_parts(out, half, both[...])
    parts = []
    for s in range(scenes):
        for q in (0, rows - 1):
            parts.append(rows_mask[0, s, pl.ds(place.row(q, rows), 1), :].astype(f32))
    columns = mask_columns(jnp.concatenate(parts, axis=0))
    size = scenes * cols
    for s in range(scenes):
        here = slice(s * cols, (s + 1) * cols)
        there = slice(size + s * cols, size + (s + 1) * cols)
        for n, edge in enumerate((near, far)):
            at = 2 * s + n
            edge[here, :] = (held[n, s].astype(f32) * columns[:, at : at + 1]).astype(bf16)
        near[there, :] = held[2, s]
        far_cot[here, :] = held[3, s]


def gather_kernel(own, gain, bias, r1, r2, r3, o1, o2, o3, weights, gbs):
    place = Place()
    taps, ch = own.shape[1:]
    piece = taps // 6

    def put(section, p, rows):
        at = (2 * place.tap(p // 2) + p % 2) * piece
        weights[section, pl.ds(pl.multiple_of(at, 16), piece), :] = rows

    for p in range(6):
        put(place.section, p, own[0, p * piece : (p + 1) * piece])
    gbs[place.section] = jnp.concatenate([gain[...], bias[...], jnp.zeros((6, ch), f32)], axis=0)
    for d, got, other in ((1, r1, o1), (2, r2, o2), (3, r3, o3)):
        there = place.section ^ d
        for n in range(3):
            rows = slice(n * piece, (n + 1) * piece)
            put(there, 3 * place.core + n, got[rows])
            put(there, 3 * (1 - place.core) + n, other[rows])
        parts = got[3 * piece :].astype(f32)
        gbs[there] = parts[0:8] + parts[8:16] + parts[16:24]


def far_kernel(rows_ref, *rest):
    *more, far = rest
    scenes, rows, cols, ch = rows_ref.shape
    for s in range(scenes):
        far[s * cols : (s + 1) * cols, :] = rows_ref[s, rows - 1].astype(bf16)
    if more:
        far[scenes * cols :, :] = more[0][...]


def finish_forward(stack, blocks, pre, near, sums, make_rows, columns, third):
    scenes, rows, cols, ch = pre.shape
    first = second = None
    make_rows(0)
    for scene in range(scenes):
        if scene + 1 < scenes:
            make_rows(scene + 1)
        for p in range(rows // 2):
            both = conv_pair(stack, None, blocks, scene, p)
            for n in range(2):
                r = 2 * p + n
                kept = row = both[:, n * ch : (n + 1) * ch]
                if columns is not None:
                    at = scene * rows + r
                    inside = columns[:, at : at + 1] > 0.5
                    kept = jnp.where(inside, row, hole)
                    row = jnp.where(inside, row, 0.0)
                pre[scene, r] = kept
                if r == 0:
                    near[scene * cols : (scene + 1) * cols, :] = kept.astype(bf16)
                first = plus(first, fold(row))
                second = plus(second, fold(row * row))
    put_sums(sums, near, sum_rows(first, second, third))


def first_kernel(mask, features, near, far, weights, x, pre, near_out, sums, stack, blocks):
    scenes, rows, cols, ch = features.shape[1:]
    put_blocks(weights.at[0], blocks)
    place = Place()
    mask_now = mask_rows(place, mask)
    columns = mask_columns(mask_now)

    def make_rows(scene):
        here = slice(scene * cols, (scene + 1) * cols)
        for k in range(rows + 2):
            if k == 0:
                value = near[here, :].astype(f32)
            elif k == rows + 1:
                value = far[here, :].astype(f32)
            else:
                at = scene * rows + k - 1
                value = features[0, scene, place.row(k - 1, rows)].astype(f32) * columns[:, at : at + 1]
            x[scene, k] = value.astype(bf16)
            put_row(stack, scene, k, value, False)

    total = jnp.sum(jnp.sum(mask_now, axis=1, keepdims=True), axis=0, keepdims=True)
    third = jnp.broadcast_to(total, (1, ch))
    finish_forward(stack, blocks, pre, near_out, sums, make_rows, columns, third)


def next_kernel(section, count, n, x_in, pre_in, near, far, *rest):
    pieces, rest = rest[:n], rest[n:]
    gbs, weights, x, pre, near_out, sums, stack, blocks = rest
    scenes, rows, cols, ch = pre.shape
    put_blocks(weights.at[section], blocks)
    scale, offset = stat_affine(pieces, count, gbs[section - 1])
    inside = Place().inside

    def make_rows(scene):
        here = slice(scene * cols, (scene + 1) * cols)
        for k in range(rows + 2):
            if k == 0:
                act = act_of(near[here, :].astype(f32), scale, offset, count)
            elif k == rows + 1:
                act = inside * act_of(far[here, :].astype(f32), scale, offset, count)
            else:
                act = act_of(pre_in[scene, k - 1], scale, offset, count)
            value = x_in[scene, k].astype(f32) + act
            x[scene, k] = value.astype(bf16)
            put_row(stack, scene, k, value, False)

    finish_forward(stack, blocks, pre, near_out, sums, make_rows, None, None)


def stat_affine(pieces, count, gb):
    mean, inv, _ = norm_stats(summed(pieces), count)
    return half_affine(mean, inv, gb)


def act_of(value, scale, offset, count):
    half = value * scale + offset
    act = half * jnp.tanh(half) + half
    return jnp.where(value > hole_edge, act, 0.0) if count is None else act


def slope_of(value, scale, offset, count):
    half = value * scale + offset
    out = twice_slope(half, jnp.tanh(half))
    return jnp.where(value > hole_edge, out, 0.0) if count is None else out


def at_scene(scene, cols):
    start = scene * cols
    return pl.ds(start if isinstance(scene, int) else pl.multiple_of(start, 16), cols)


def slope_kernel(section, count, n, pre, near, *rest):
    pieces, (gbs, slope) = rest[:n], rest[n:]
    scenes, padded, cols, ch = slope.shape
    scale, offset = stat_affine(pieces, count, gbs[section])

    @pl.loop(0, scenes)
    def _(scene):
        for k in range(padded):
            value = pre[scene, k - 1] if k else near[at_scene(scene, cols), :].astype(f32)
            slope[scene, k] = slope_of(value, scale, offset, count)


def turn_kernel(count, n, section, pre, cot, *rest):
    pieces, (gbs, grad_u, sums) = rest[:n], rest[n:]
    scenes, rows, cols, ch = grad_u.shape
    mean, inv, _ = norm_stats(summed(pieces), count)
    scale, offset = half_affine(mean, inv, gbs[section])
    place = Place()

    def one(scene, total):
        first, second = total
        for q in range(rows):
            value = pre[scene, q]
            grad = cot[0, scene, place.row(q, rows)].astype(f32) * slope_of(value, scale, offset, count)
            grad_u[scene, q] = grad
            first = first + fold(grad * value)
            second = second + fold(grad)
        return first, second

    zero = jnp.zeros((8, ch), f32)
    first, second = lax.fori_loop(0, scenes, one, (zero, zero))
    put_sums(sums, None, grad_sums(first, second, mean, inv))


def grad_sums(by_pre, plain, mean, inv):
    by_pre = 0.5 * jnp.sum(by_pre, axis=0, keepdims=True)
    plain = 0.5 * jnp.sum(plain, axis=0, keepdims=True)
    return jnp.concatenate(
        [inv * (by_pre - mean * plain), plain, jnp.zeros((6, plain.shape[1]), f32)], axis=0
    )


def neck_kernel(count, n, section, x, pre, *rest):
    pieces, (gbs, neck) = rest[:n], rest[n:]
    scenes, rows = neck.shape[1:3]
    scale, offset = stat_affine(pieces, count, gbs[section])
    place = Place()

    @pl.loop(0, scenes)
    def _(scene):
        for q in range(rows):
            act = act_of(pre[scene, q], scale, offset, count)
            neck[0, scene, place.row(q, rows)] = (x[scene, q + 1].astype(f32) + act).astype(bf16)


def back_terms(section, count, pieces, grads, gbs):
    mean, inv, cells = norm_stats(summed(pieces), count)
    total = summed(grads)
    lead = inv * gbs[section][0:1]
    by_pre = -lead * inv * total[0:1] / cells
    constant = -lead * total[1:2] / cells - by_pre * mean
    return (0.5 * lead, by_pre, constant), total


def grad_pre(terms, lifted, value, count):
    lead, by_pre, constant = terms
    out = lead * lifted + (by_pre * value + constant)
    return jnp.where(value > hole_edge, out, 0.0) if count is None else out


def back_rows(count, last, terms, stack, grad_u, g1, pre, p1, slope):
    scenes, rows, cols, ch = grad_u.shape
    base = scenes * cols if last else 0

    def make_rows(scene):
        at = scene * cols
        for k in range(rows + 1):
            if k:
                value = pre[scene, k - 1]
                lifted = grad_u[scene, k - 1]
            else:
                value = p1[at : at + cols, :].astype(f32)
                lifted = g1[base + at : base + at + cols, :].astype(f32) * slope[scene, 0]
            put_row(stack, scene, k, grad_pre(terms, lifted, value, count), True)

    return make_rows


def back_outer_row(section, count, last, terms, g2, p2, pieces, gbs, cols):
    base = p2.shape[0] // 2 if last else 0
    scale, offset = stat_affine(pieces, count, gbs[section])
    inside = Place().inside

    def outer_row(scene):
        at = at_scene(scene, cols)
        value = p2[at, :].astype(f32)
        lifted = g2[pl.ds(base + at.start, cols), :].astype(f32) * slope_of(value, scale, offset, count)
        return inside * grad_pre(terms, lifted, value, count)

    return outer_row


def grad_row(grad_in, last, scene, q, rows):
    return grad_in[0, scene, Place().row(q, rows)] if last else grad_in[scene, q]


def back_kernel(section, count, count_below, last, n, *rest):
    pieces, rest = rest[:n], rest[n:]
    grads, rest = rest[:n], rest[n:]
    pieces_below, rest = rest[:n], rest[n:]
    pre_below, slope_below, grad_u, grad_in, g1, g2, pre, p1, p2, slope, gbs, weights, *rest = rest
    stack, grad_out, grad_u_below, near, sums, total_out, blocks = rest
    scenes, rows, cols, ch = grad_u.shape
    put_blocks(weights.at[section], blocks)
    terms, total = back_terms(section, count, pieces, grads, gbs)
    total_out[...] = total
    mean_below, inv_below, _ = norm_stats(summed(pieces_below), count_below)
    make_rows = back_rows(count, last, terms, stack, grad_u, g1, pre, p1, slope)
    outer_row = back_outer_row(section, count, last, terms, g2, p2, pieces, gbs, cols)

    def make_all(scene):
        make_rows(scene)
        put_row(stack, scene, rows + 1, outer_row(scene), True)

    first = second = None
    make_all(0)
    for scene in range(scenes):
        if scene + 1 < scenes:
            make_all(scene + 1)
        for p in range(rows // 2):
            both = conv_back_pair(stack, None, blocks, scene, p)
            for m in range(2):
                r = 2 * p + m
                grad = grad_row(grad_in, last, scene, r, rows).astype(f32)
                grad = (grad + both[:, m * ch : (m + 1) * ch]).astype(bf16)
                grad_out[scene, r] = grad
                if r == 0:
                    near[scene * cols : (scene + 1) * cols, :] = grad
                lifted = grad.astype(f32) * slope_below[scene, r + 1]
                grad_u_below[scene, r] = lifted
                first = plus(first, fold(lifted * pre_below[scene, r]))
                second = plus(second, fold(lifted))
    put_sums(sums, near, grad_sums(first, second, mean_below, inv_below))


def final_weight_kernel(section, count, last, n, *rest):
    pieces, rest = rest[:n], rest[n:]
    grads, rest = rest[:n], rest[n:]
    grad_u, g1, pre, p1, slope, gbs, x, stack, mine, theirs, total_out, whole = rest
    terms, total = back_terms(section, count, pieces, grads, gbs)
    total_out[...] = total
    make_rows = back_rows(count, last, terms, stack, grad_u, g1, pre, p1, slope)
    weight_body(x, stack, mine, theirs, whole, make_rows)


def final_grad_kernel(section, count, last, n, *rest):
    pieces, rest = rest[:n], rest[n:]
    grads, rest = rest[:n], rest[n:]
    grad_in, g2, pre, p2, gbs, weights, stack, grad_out, outer, blocks = rest
    scenes, rows, cols, ch = grad_out.shape[1:]
    put_blocks(weights.at[section], blocks)
    terms, _ = back_terms(section, count, pieces, grads, gbs)
    outer_row = back_outer_row(section, count, last, terms, g2, p2, pieces, gbs, cols)
    place = Place()

    @pl.loop(0, scenes)
    def _(scene):
        put_outer(outer, scene, outer_row(scene), True)
        for p in range(rows // 2):
            both = conv_back_pair(stack, outer, blocks, scene, p)
            for m in range(2):
                r = 2 * p + m
                grad = grad_row(grad_in, last, scene, r, rows).astype(f32)
                grad = grad + both[:, m * ch : (m + 1) * ch]
                if count is None:
                    grad = jnp.where(pre[scene, r] > hole_edge, grad, 0.0)
                grad_out[0, scene, place.row(r, rows)] = grad.astype(bf16)


def weight_kernel(x, stack, mine, theirs, whole):
    weight_body(x, stack, mine, theirs, whole, None)


def weight_body(x, stack, mine, theirs, whole, make_rows):
    scenes, padded, cols, ch = x.shape
    rows = padded - 2
    place = Place()
    total = None
    if make_rows:
        make_rows(0)
    for scene in range(scenes):
        if make_rows and scene + 1 < scenes:
            make_rows(scene + 1)
        lines = [x[scene, k] for k in range(rows + 2)]
        lhs = jnp.concatenate(
            [jnp.concatenate(lines[i : i + rows], axis=0) for i in range(3)], axis=1
        )
        rhs = jnp.concatenate(
            [
                jnp.concatenate(
                    [
                        stack[j, k // 2, scene, :, (k % 2) * ch : (k % 2 + 1) * ch]
                        for j in range(3)
                    ],
                    axis=1,
                )
                for k in range(1, rows + 1)
            ],
            axis=0,
        )
        term = lax.dot_general(lhs, rhs, (((0,), (0,)), ((), ())), preferred_element_type=f32)
        total = plus(total, term)
    for i in range(3):
        for j in range(3):
            at = pl.multiple_of((3 * place.tap(i) + j) * ch, 8)
            whole[pl.ds(at, ch), :] = total[i * ch : (i + 1) * ch, j * ch : (j + 1) * ch]
    chips, chunk = mine.shape[:2]
    for z in range(chips):
        at = pl.multiple_of((2 * z + place.core) * chunk, 8)
        mine[z] = whole[pl.ds(at, chunk), :]
        at = pl.multiple_of((2 * z + 1 - place.core) * chunk, 8)
        theirs[z] = whole[pl.ds(at, chunk), :].astype(bf16)


def chip_kernel(n, *refs):
    mine, refs = refs[:n], refs[n:]
    theirs, refs = refs[:n], refs[n:]
    totals, refs = refs[:n], refs[n:]
    outs, held, sums = refs[:4], refs[4], refs[5]
    here = Place().section
    chips, chunk, ch = mine[0].shape
    for s in range(n):
        for z in range(chips):
            held[s, z * chunk : (z + 1) * chunk] = mine[s][z] + theirs[s][z].astype(f32)
        sums[s] = totals[s][...]
    size = chips * chunk
    for d in range(4):
        if d:
            outs[d][:size] = held[here ^ d].astype(bf16)
            put_parts(outs[d], size, sums[here ^ d])
        else:
            outs[0][:size] = held[here]
            outs[0][size:] = sums[here]


def section_kernel(own, a, b, c, mine, one, two, three, sums, held):
    chips, chunk = held.shape[:2]
    size = chips * chunk
    for z in range(chips):
        at = slice(z * chunk, (z + 1) * chunk)
        held[z] = own[at] + a[at].astype(f32) + b[at].astype(f32) + c[at].astype(f32)
    total = own[size:]
    for got in (a, b, c):
        parts = got[size:].astype(f32)
        total = total + (parts[0:8] + parts[8:16] + parts[16:24])
    sums[...] = total
    chip = Place().chip
    mine[...] = held[chip]
    for k, out in ((1, one), (2, two), (3, three)):
        out[...] = held[chip ^ k].astype(bf16)


def last_kernel(mine, a, b, c, sums, weight, gain, bias):
    gain[...] = sums[0:1]
    bias[...] = sums[1:2]
    weight[0] = mine[...] + a[...].astype(f32) + b[...].astype(f32) + c[...].astype(f32)


def call(body, outs, ins, scratch=(), flops=0, name=None, hbm=()):
    specs = [VMEM_SPEC] * len(ins)
    for n in hbm:
        specs[n] = pl.BlockSpec(memory_space=pltpu.HBM)
    return pl.pallas_call(
        body,
        out_shape=[jax.ShapeDtypeStruct(s, d) for s, d in outs],
        in_specs=specs,
        out_specs=[VMEM_SPEC] * len(outs),
        scratch_shapes=list(scratch),
        compiler_params=pltpu.CompilerParams(vmem_limit_bytes=12 * 2**20),
        cost_estimate=pl.CostEstimate(flops=flops, bytes_accessed=0, transcendentals=0),
        name=name,
    )(*ins)


def swap(value, axis, step):
    count = lax.axis_size(axis)
    return lax.ppermute(value, axis, [(i, i ^ step) for i in range(count)])


def swap_next(value):
    pairs = []
    for i in range(1, lax.axis_size("row") - 1, 2):
        pairs += [(i, i + 1), (i + 1, i)]
    return lax.ppermute(value, "row", pairs)


def row_pieces(total):
    count = lax.axis_size("row")
    stride = 2
    while True:
        group = min(4, count // stride)
        pieces = [total] + [swap(total, "row", k * stride + (stride == 2)) for k in range(1, group)]
        stride *= group
        if stride >= count:
            return pieces
        total = sum(pieces[1:], pieces[0])


def after(value, signal):
    return lax.optimization_barrier((value, signal))[0]


def far_rows(rows_ref, *more):
    scenes, _, cols, ch = rows_ref.shape
    size = scenes * cols * (1 + len(more))
    (far,) = call(far_kernel, [((size, ch), bf16)], (rows_ref, *more), name="far")
    return far


def exchange(sums, near, rows_ref=None):
    got = swap(near, "row", 1)
    far = None if rows_ref is None else swap_next(far_rows(rows_ref))
    parts = got[got.shape[0] - 32 :].astype(f32)
    total = sums + (parts[0:8] + parts[8:16] + parts[16:24])
    return got, far, row_pieces(total), total


def per_device(features, conv_weight, norm_gain, norm_bias, valid_mask, out_cotangent):
    sections = lax.axis_size("section")
    tiles = lax.axis_size("row")
    scenes, rows, cols, ch = features.shape[1:]
    taps = conv_weight.shape[1]
    cells = float(scenes * rows * cols * tiles)
    tile_shape = (scenes, rows, cols, ch)
    pad_shape = (scenes, rows + 2, cols, ch)
    slope_shape = (scenes, rows + 1, cols, ch)
    edge = scenes * cols
    near_shape = (edge + 32, ch)
    sum_shape = (8, ch)
    stack_shape = (3, rows // 2 + 1, scenes, cols, 2 * ch)
    blocks = pltpu.VMEM((6, 2 * ch, 2 * ch), bf16)
    outer = pltpu.VMEM((3, scenes, cols, ch), bf16)
    flops = 2 * scenes * rows * cols * taps * ch
    half = taps // 2
    chunk = taps // tiles
    direct = tiles == 8 and chunk % 16 == 0

    def in_hbm(*values):
        return [pltpu.with_memory_space_constraint(v, pltpu.HBM) for v in values]

    e1, e2, cot_far, wsend = call(
        prep_kernel,
        [((2 * edge, ch), bf16), ((edge, ch), bf16), ((edge, ch), bf16), ((half + 32, ch), bf16)],
        in_hbm(valid_mask, features, out_cotangent, conv_weight, norm_gain, norm_bias),
        [
            pltpu.VMEM((4, scenes, cols, ch), bf16),
            pltpu.VMEM((1, scenes, rows, cols), jnp.int32),
            pltpu.VMEM((8, ch), f32),
            pltpu.SemaphoreType.DMA((8,)),
        ],
        hbm=range(6),
        name="prep",
    )
    got = [swap(wsend, "section", d) for d in (1, 2, 3)]
    e1 = swap(e1, "row", 1)
    e2 = swap_next(e2)
    got[1] = after(got[1], e1)
    others = [swap(v, "row", 1) for v in got]
    weights, gbs = call(
        gather_kernel,
        [((sections, taps, ch), bf16), ((sections, 8, ch), f32)],
        (conv_weight, norm_gain, norm_bias, *got, *others),
        name="gather",
    )

    forward_outs = [(pad_shape, bf16), (tile_shape, f32), (near_shape, bf16), (sum_shape, f32)]
    scratch = [pltpu.VMEM(stack_shape, bf16), blocks]
    kept = []
    slopes = []
    x, pre, near, sums = call(
        first_kernel,
        forward_outs,
        (valid_mask, features, e1, e2, weights),
        scratch,
        flops=flops,
        name="forward",
    )
    for section in range(sections):
        count = None if section == 0 else cells
        last = section == sections - 1
        near, far, pieces, total = exchange(sums, near, None if last else pre)
        if last:
            far = swap_next(far_rows(after(pre, total), cot_far))
        if section > 0:
            _, below, below_near, _, below_pieces, below_count = kept[-1]
            slopes += call(
                functools.partial(slope_kernel, section - 1, below_count, len(pieces)),
                [(slope_shape, f32)],
                (after(below, total), below_near, *below_pieces, gbs),
                flops=8 * flops if last else 0,
                name="slope",
            )
            pieces[0] = after(pieces[0], slopes[-1])
        kept.append((x, pre, near, far, pieces, count))
        if section == sections - 1:
            break
        x, pre, near, sums = call(
            functools.partial(next_kernel, section + 1, count, len(pieces)),
            forward_outs,
            (x, pre, near, far, *pieces, gbs, weights),
            scratch,
            flops=flops,
            name="forward",
        )
    n = len(pieces)
    grad_u, sums = call(
        functools.partial(turn_kernel, count, n, sections - 1),
        [(tile_shape, f32), (sum_shape, f32)],
        (pre, out_cotangent, *pieces, gbs),
        name="turn",
    )
    total = sums + swap(sums, "row", 1)
    grads = row_pieces(total)
    slopes += call(
        functools.partial(slope_kernel, sections - 1, count, n),
        [(slope_shape, f32)],
        (after(pre, total), near, *pieces, gbs),
        name="slope",
    )
    grad, g1, g2 = out_cotangent, e1, far
    parts = [None] * sections
    totals = [None] * sections
    part_shapes = [((tiles // 2, chunk, ch), f32), ((tiles // 2, chunk, ch), bf16)]
    whole = pltpu.VMEM((taps, ch), f32)
    for section in range(sections - 1, 0, -1):
        x, pre, p1, p2, pieces, count = kept[section]
        _, below, _, _, below_pieces, below_count = kept[section - 1]
        last = section == sections - 1
        stack, grad, grad_u, near, sums, totals[section] = call(
            functools.partial(back_kernel, section, count, below_count, last, n),
            [
                (stack_shape, bf16),
                (tile_shape, bf16),
                (tile_shape, f32),
                (near_shape, bf16),
                (sum_shape, f32),
                (sum_shape, f32),
            ],
            (
                *pieces,
                *grads,
                *below_pieces,
                below,
                slopes[section - 1],
                grad_u,
                grad,
                g1,
                g2,
                pre,
                p1,
                p2,
                slopes[section],
                gbs,
                weights,
            ),
            [blocks],
            flops=flops,
            name="backward",
        )
        g1, g2, grads, total = exchange(sums, near, grad if section > 1 else None)
        parts[section] = call(
            weight_kernel,
            part_shapes,
            (x, after(stack, total)),
            [whole],
            flops=flops,
            name="weight",
        )
        grads[0] = after(grads[0], parts[section][1])
    x, pre, p1, p2, pieces, count = kept[0]
    last = sections == 1
    stack, *parts[0], totals[0] = call(
        functools.partial(final_weight_kernel, 0, count, last, n),
        [(stack_shape, bf16), *part_shapes, (sum_shape, f32)],
        (*pieces, *grads, grad_u, g1, pre, p1, slopes[0], gbs, x),
        [whole],
        flops=flops,
        name="weight",
    )

    def finish_neck(signal):
        far = swap_next(far_rows(after(grad, signal)))
        last_x, last_pre, _, _, last_pieces, last_count = kept[-1]
        (neck,) = call(
            functools.partial(neck_kernel, last_count, n, sections - 1),
            [((1,) + tile_shape, bf16)],
            (last_x, after(last_pre, signal), *last_pieces, gbs),
            flops=8 * flops,
            name="neck",
        )
        return neck, far

    def finish_grad(far, signal):
        (feature_grad,) = call(
            functools.partial(final_grad_kernel, 0, count, last, n),
            [((1,) + tile_shape, bf16)],
            (*pieces, *grads, grad, far, pre, p2, gbs, weights, after(stack, signal)),
            [outer, blocks],
            flops=flops,
            name="final_grad",
        )
        return feature_grad

    m = sections
    if direct:
        size = taps // 2
        theirs = [swap(p[1], "row", 1) for p in parts]
        own, *sending = call(
            functools.partial(chip_kernel, m),
            [((size + 8, ch), f32)] + [((size + 32, ch), bf16)] * 3,
            (*[p[0] for p in parts], *theirs, *totals),
            [pltpu.VMEM((m, size, ch), f32), pltpu.VMEM((m, 8, ch), f32)],
            name="chips",
        )
        received = [swap(v, "section", d + 1) for d, v in enumerate(sending)]
        neck, far = finish_neck(own)
        received[0] = after(received[0], neck)
        mine, one, two, three, total = call(
            section_kernel,
            [((chunk, ch), f32)] + [((chunk, ch), bf16)] * 3 + [(sum_shape, f32)],
            (own, *received),
            [pltpu.VMEM((tiles // 2, chunk, ch), f32)],
            name="sections",
        )
        chunks = [swap(v, "row", 2 * (k + 1)) for k, v in enumerate((one, two, three))]
        feature_grad = finish_grad(far, total)
        mine = after(mine, feature_grad)
        weight_grad, gain_grad, bias_grad = call(
            last_kernel,
            [((1, chunk, ch), f32), ((1, ch), f32), ((1, ch), f32)],
            (mine, *chunks, total),
            name="last",
        )
    else:
        lanes = [list(range(c, tiles, 2)) for c in range(2)]
        here = lax.axis_index("section")
        chip_sums = jnp.stack([p[0] + swap(p[1], "row", 1).astype(f32) for p in parts])
        sums = jnp.stack(totals)

        def over_sections(stacked):
            total, *others = [
                lax.dynamic_index_in_dim(stacked, here ^ d, 0, keepdims=False) for d in range(4)
            ]
            for d, other in enumerate(others):
                total = total + swap(other, "section", d + 1)
            return total

        chip_sum, total = over_sections(chip_sums), over_sections(sums)
        weight_grad = lax.psum_scatter(
            chip_sum, "row", scatter_dimension=0, tiled=True, axis_index_groups=lanes
        )
        gain_grad, bias_grad = total[0:1], total[1:2]
        neck, far = finish_neck(total)
        feature_grad = finish_grad(far, neck)
    return neck, feature_grad, weight_grad, gain_grad, bias_grad


def solution(mesh):
    return jax.shard_map(
        per_device,
        mesh=mesh,
        in_specs=(
            P("section", None, "row", None, None),
            P("section", None, None),
            P("section", None),
            P("section", None),
            P(None, None, "row", None),
            P("section", None, "row", None, None),
        ),
        out_specs=(
            P("section", None, "row", None, None),
            P("section", None, "row", None, None),
            P("section", "row", None),
            P("section", None),
            P("section", None),
        ),
        check_vma=False,
    )
```

```python
import functools

import jax
import jax.numpy as jnp
from jax import lax
from jax.experimental import pallas as pl
from jax.experimental.pallas import tpu as pltpu
from jax.sharding import PartitionSpec as P

norm_eps = 1e-05
hole = -1e30
hole_edge = -1e29
f32 = jnp.float32
bf16 = jnp.bfloat16
VMEM_SPEC = pl.BlockSpec(memory_space=pltpu.VMEM)


class Place:
    def __init__(self):
        tile = lax.axis_index("row")
        self.section = lax.axis_index("section")
        self.core = lax.rem(tile, 2)
        self.even = self.core == 0
        self.chip = tile // 2
        outer = jnp.where(self.even, 0, lax.axis_size("row") - 1)
        self.inside = (tile != outer).astype(f32)

    def row(self, q, rows):
        return jnp.where(self.even, rows - 1 - q, q)

    def tap(self, i):
        return jnp.where(self.even, 2 - i, i)


def shifted(value, step):
    cols = value.shape[0]
    index = lax.broadcasted_iota(jnp.int32, value.shape, 0)
    edge = 0 if step == 1 else cols - 1
    return jnp.where(index == edge, 0.0, pltpu.roll(value, step % cols, 0))


def shifts(value, flip):
    left, right = shifted(value, 1).astype(bf16), shifted(value, -1).astype(bf16)
    return (right, value.astype(bf16), left) if flip else (left, value.astype(bf16), right)


def put_row(stack, scene, k, value, flip):
    ch = value.shape[1]
    for j, part in enumerate(shifts(value, flip)):
        stack[j, k // 2, scene, :, (k % 2) * ch : (k % 2 + 1) * ch] = part


def put_outer(outer, scene, value, flip):
    for j, part in enumerate(shifts(value, flip)):
        outer[j, scene] = part


def put_blocks(kernel_rows, blocks):
    ch = kernel_rows.shape[1]

    def tap(i, j):
        return kernel_rows[(3 * i + j) * ch : (3 * i + j + 1) * ch, :]

    zero = jnp.zeros((ch, ch), bf16)
    for j in range(3):
        blocks[2 * j, :ch, :ch] = tap(0, j)
        blocks[2 * j, :ch, ch:] = zero
        blocks[2 * j, ch:, :ch] = tap(1, j)
        blocks[2 * j, ch:, ch:] = tap(0, j)
        blocks[2 * j + 1, :ch, :ch] = tap(2, j)
        blocks[2 * j + 1, :ch, ch:] = tap(1, j)
        blocks[2 * j + 1, ch:, :ch] = zero
        blocks[2 * j + 1, ch:, ch:] = tap(2, j)


def operand(stack, outer, scene, j, pair):
    if outer is None or pair + 1 < stack.shape[1]:
        return stack[j, pair, scene]
    ch = outer.shape[-1]
    return jnp.concatenate([stack[j, pair, scene, :, :ch], outer[j, scene]], axis=1)


def conv_pair(stack, outer, blocks, scene, p):
    lhs = [operand(stack, outer, scene, j, p + h) for j in range(3) for h in range(2)]
    rhs = jnp.concatenate([blocks[n] for n in range(6)], axis=0)
    return jnp.dot(jnp.concatenate(lhs, axis=1), rhs, preferred_element_type=f32)


def conv_back_pair(stack, outer, blocks, scene, p):
    total = None
    for j in range(3):
        for h in range(2):
            term = lax.dot_general(
                operand(stack, outer, scene, j, p + h),
                blocks[2 * j + 1 - h],
                (((1,), (1,)), ((), ())),
                preferred_element_type=f32,
            )
            total = term if total is None else total + term
    return total


def summed(pieces):
    total = pieces[0][...]
    for piece in pieces[1:]:
        total = total + piece[...]
    return total


def norm_stats(total, count):
    count = total[2:3] if count is None else count
    mean = total[0:1] / count
    inv = lax.rsqrt(total[1:2] / count - mean * mean + norm_eps)
    return mean, inv, count


def half_affine(mean, inv, gb):
    scale = inv * gb[0:1]
    return 0.5 * scale, 0.5 * (gb[1:2] - mean * scale)


def twice_slope(half, t):
    return (1.0 + t) + half * (1.0 - t * t)


def fold(value):
    return jnp.sum(value.reshape(-1, 8, value.shape[-1]), axis=0)


def plus(total, term):
    return term if total is None else total + term


def sum_rows(first, second, third=None):
    ch = first.shape[1]
    rows = [jnp.sum(first, axis=0, keepdims=True), jnp.sum(second, axis=0, keepdims=True)]
    rows.append(jnp.zeros((1, ch), f32) if third is None else third)
    return jnp.concatenate(rows + [jnp.zeros((5, ch), f32)], axis=0)


def put_parts(out, start, total):
    hi = total.astype(bf16).astype(f32)
    left = total - hi
    mid = left.astype(bf16).astype(f32)
    parts = [hi, mid, left - mid, jnp.zeros_like(total)]
    out[start : start + 16, :] = jnp.concatenate(parts[:2], axis=0).astype(bf16)
    out[start + 16 : start + 32, :] = jnp.concatenate(parts[2:], axis=0).astype(bf16)


def put_sums(sums, near, total):
    sums[...] = total
    if near is not None:
        put_parts(near, near.shape[0] - 32, total)


def mask_columns(rows):
    count, cols = rows.shape
    filled = jnp.concatenate([rows, jnp.zeros((128 - count, cols), f32)], axis=0)
    return filled.T


def mask_rows(place, mask):
    scenes, rows = mask.shape[1:3]
    parts = []
    for s in range(scenes):
        parts += [mask[place.section, s, pl.ds(place.row(q, rows), 1), :].astype(f32) for q in range(rows)]
    return jnp.concatenate(parts, axis=0)


def prep_kernel(mask, features, cot, weight, gain, bias, near, far, far_cot, out, held, rows_mask, both, sems):
    place = Place()
    scenes, rows, cols, ch = features.shape[1:]
    half = weight.shape[1] // 2
    mine = pl.ds(pl.multiple_of(place.core * half, 16), half)
    moves = [
        (weight.at[0, mine], out.at[pl.ds(0, half)]),
        (gain, both.at[pl.ds(0, 1)]),
        (bias, both.at[pl.ds(1, 1)]),
        (mask.at[pl.ds(place.section, 1)], rows_mask),
    ]
    for source in (features, cot):
        for q in (0, rows - 1):
            moves.append((source.at[0, :, place.row(q, rows)], held.at[len(moves) - 4]))
    copies = [pltpu.make_async_copy(a, b, sems.at[n]) for n, (a, b) in enumerate(moves)]
    for copy in copies:
        copy.start()
    both[2:8] = jnp.zeros((6, ch), f32)
    for copy in copies:
        copy.wait()
    put_parts(out, half, both[...])
    parts = []
    for s in range(scenes):
        for q in (0, rows - 1):
            parts.append(rows_mask[0, s, pl.ds(place.row(q, rows), 1), :].astype(f32))
    columns = mask_columns(jnp.concatenate(parts, axis=0))
    size = scenes * cols
    for s in range(scenes):
        here = slice(s * cols, (s + 1) * cols)
        there = slice(size + s * cols, size + (s + 1) * cols)
        for n, edge in enumerate((near, far)):
            at = 2 * s + n
            edge[here, :] = (held[n, s].astype(f32) * columns[:, at : at + 1]).astype(bf16)
        near[there, :] = held[2, s]
        far_cot[here, :] = held[3, s]


def gather_kernel(own, gain, bias, r1, r2, r3, o1, o2, o3, weights, gbs):
    place = Place()
    taps, ch = own.shape[1:]
    piece = taps // 6

    def put(section, p, rows):
        at = (2 * place.tap(p // 2) + p % 2) * piece
        weights[section, pl.ds(pl.multiple_of(at, 16), piece), :] = rows

    for p in range(6):
        put(place.section, p, own[0, p * piece : (p + 1) * piece])
    gbs[place.section] = jnp.concatenate([gain[...], bias[...], jnp.zeros((6, ch), f32)], axis=0)
    for d, got, other in ((1, r1, o1), (2, r2, o2), (3, r3, o3)):
        there = place.section ^ d
        for n in range(3):
            rows = slice(n * piece, (n + 1) * piece)
            put(there, 3 * place.core + n, got[rows])
            put(there, 3 * (1 - place.core) + n, other[rows])
        parts = got[3 * piece :].astype(f32)
        gbs[there] = parts[0:8] + parts[8:16] + parts[16:24]


def far_kernel(rows_ref, *rest):
    *more, far = rest
    scenes, rows, cols, ch = rows_ref.shape
    for s in range(scenes):
        far[s * cols : (s + 1) * cols, :] = rows_ref[s, rows - 1].astype(bf16)
    if more:
        far[scenes * cols :, :] = more[0][...]


def finish_forward(stack, blocks, pre, near, sums, make_rows, columns, third):
    scenes, rows, cols, ch = pre.shape
    first = second = None
    make_rows(0)
    for scene in range(scenes):
        if scene + 1 < scenes:
            make_rows(scene + 1)
        for p in range(rows // 2):
            both = conv_pair(stack, None, blocks, scene, p)
            for n in range(2):
                r = 2 * p + n
                kept = row = both[:, n * ch : (n + 1) * ch]
                if columns is not None:
                    at = scene * rows + r
                    inside = columns[:, at : at + 1] > 0.5
                    kept = jnp.where(inside, row, hole)
                    row = jnp.where(inside, row, 0.0)
                pre[scene, r] = kept
                if r == 0:
                    near[scene * cols : (scene + 1) * cols, :] = kept.astype(bf16)
                first = plus(first, fold(row))
                second = plus(second, fold(row * row))
    put_sums(sums, near, sum_rows(first, second, third))


def first_kernel(mask, features, near, far, weights, x, pre, near_out, sums, stack, blocks):
    scenes, rows, cols, ch = features.shape[1:]
    put_blocks(weights.at[0], blocks)
    place = Place()
    mask_now = mask_rows(place, mask)
    columns = mask_columns(mask_now)

    def make_rows(scene):
        here = slice(scene * cols, (scene + 1) * cols)
        for k in range(rows + 2):
            if k == 0:
                value = near[here, :].astype(f32)
            elif k == rows + 1:
                value = far[here, :].astype(f32)
            else:
                at = scene * rows + k - 1
                value = features[0, scene, place.row(k - 1, rows)].astype(f32) * columns[:, at : at + 1]
            x[scene, k] = value.astype(bf16)
            put_row(stack, scene, k, value, False)

    total = jnp.sum(jnp.sum(mask_now, axis=1, keepdims=True), axis=0, keepdims=True)
    third = jnp.broadcast_to(total, (1, ch))
    finish_forward(stack, blocks, pre, near_out, sums, make_rows, columns, third)


def next_kernel(section, count, n, x_in, pre_in, near, far, *rest):
    pieces, rest = rest[:n], rest[n:]
    gbs, weights, x, pre, near_out, sums, stack, blocks = rest
    scenes, rows, cols, ch = pre.shape
    put_blocks(weights.at[section], blocks)
    scale, offset = stat_affine(pieces, count, gbs[section - 1])
    inside = Place().inside

    def make_rows(scene):
        here = slice(scene * cols, (scene + 1) * cols)
        for k in range(rows + 2):
            if k == 0:
                act = act_of(near[here, :].astype(f32), scale, offset, count)
            elif k == rows + 1:
                act = inside * act_of(far[here, :].astype(f32), scale, offset, count)
            else:
                act = act_of(pre_in[scene, k - 1], scale, offset, count)
            value = x_in[scene, k].astype(f32) + act
            x[scene, k] = value.astype(bf16)
            put_row(stack, scene, k, value, False)

    finish_forward(stack, blocks, pre, near_out, sums, make_rows, None, None)


def stat_affine(pieces, count, gb):
    mean, inv, _ = norm_stats(summed(pieces), count)
    return half_affine(mean, inv, gb)


def act_of(value, scale, offset, count):
    half = value * scale + offset
    act = half * jnp.tanh(half) + half
    return jnp.where(value > hole_edge, act, 0.0) if count is None else act


def slope_of(value, scale, offset, count):
    half = value * scale + offset
    out = twice_slope(half, jnp.tanh(half))
    return jnp.where(value > hole_edge, out, 0.0) if count is None else out


def at_scene(scene, cols):
    start = scene * cols
    return pl.ds(start if isinstance(scene, int) else pl.multiple_of(start, 16), cols)


def slope_kernel(section, count, n, pre, near, *rest):
    pieces, (gbs, slope) = rest[:n], rest[n:]
    scenes, padded, cols, ch = slope.shape
    scale, offset = stat_affine(pieces, count, gbs[section])

    @pl.loop(0, scenes)
    def _(scene):
        for k in range(padded):
            value = pre[scene, k - 1] if k else near[at_scene(scene, cols), :].astype(f32)
            slope[scene, k] = slope_of(value, scale, offset, count)


def turn_kernel(count, n, section, pre, cot, *rest):
    pieces, (gbs, grad_u, sums) = rest[:n], rest[n:]
    scenes, rows, cols, ch = grad_u.shape
    mean, inv, _ = norm_stats(summed(pieces), count)
    scale, offset = half_affine(mean, inv, gbs[section])
    place = Place()

    def one(scene, total):
        first, second = total
        for q in range(rows):
            value = pre[scene, q]
            grad = cot[0, scene, place.row(q, rows)].astype(f32) * slope_of(value, scale, offset, count)
            grad_u[scene, q] = grad
            first = first + fold(grad * value)
            second = second + fold(grad)
        return first, second

    zero = jnp.zeros((8, ch), f32)
    first, second = lax.fori_loop(0, scenes, one, (zero, zero))
    put_sums(sums, None, grad_sums(first, second, mean, inv))


def grad_sums(by_pre, plain, mean, inv):
    by_pre = 0.5 * jnp.sum(by_pre, axis=0, keepdims=True)
    plain = 0.5 * jnp.sum(plain, axis=0, keepdims=True)
    return jnp.concatenate(
        [inv * (by_pre - mean * plain), plain, jnp.zeros((6, plain.shape[1]), f32)], axis=0
    )


def neck_kernel(count, n, section, x, pre, *rest):
    pieces, (gbs, neck) = rest[:n], rest[n:]
    scenes, rows = neck.shape[1:3]
    scale, offset = stat_affine(pieces, count, gbs[section])
    place = Place()

    @pl.loop(0, scenes)
    def _(scene):
        for q in range(rows):
            act = act_of(pre[scene, q], scale, offset, count)
            neck[0, scene, place.row(q, rows)] = (x[scene, q + 1].astype(f32) + act).astype(bf16)


def back_terms(section, count, pieces, grads, gbs):
    mean, inv, cells = norm_stats(summed(pieces), count)
    total = summed(grads)
    lead = inv * gbs[section][0:1]
    by_pre = -lead * inv * total[0:1] / cells
    constant = -lead * total[1:2] / cells - by_pre * mean
    return (0.5 * lead, by_pre, constant), total


def grad_pre(terms, lifted, value, count):
    lead, by_pre, constant = terms
    out = lead * lifted + (by_pre * value + constant)
    return jnp.where(value > hole_edge, out, 0.0) if count is None else out


def back_rows(count, last, terms, stack, grad_u, g1, pre, p1, slope):
    scenes, rows, cols, ch = grad_u.shape
    base = scenes * cols if last else 0

    def make_rows(scene):
        at = scene * cols
        for k in range(rows + 1):
            if k:
                value = pre[scene, k - 1]
                lifted = grad_u[scene, k - 1]
            else:
                value = p1[at : at + cols, :].astype(f32)
                lifted = g1[base + at : base + at + cols, :].astype(f32) * slope[scene, 0]
            put_row(stack, scene, k, grad_pre(terms, lifted, value, count), True)

    return make_rows


def back_outer_row(section, count, last, terms, g2, p2, pieces, gbs, cols):
    base = p2.shape[0] // 2 if last else 0
    scale, offset = stat_affine(pieces, count, gbs[section])
    inside = Place().inside

    def outer_row(scene):
        at = at_scene(scene, cols)
        value = p2[at, :].astype(f32)
        lifted = g2[pl.ds(base + at.start, cols), :].astype(f32) * slope_of(value, scale, offset, count)
        return inside * grad_pre(terms, lifted, value, count)

    return outer_row


def grad_row(grad_in, last, scene, q, rows):
    return grad_in[0, scene, Place().row(q, rows)] if last else grad_in[scene, q]


def back_kernel(section, count, count_below, last, n, *rest):
    pieces, rest = rest[:n], rest[n:]
    grads, rest = rest[:n], rest[n:]
    pieces_below, rest = rest[:n], rest[n:]
    pre_below, slope_below, grad_u, grad_in, g1, g2, pre, p1, p2, slope, gbs, weights, *rest = rest
    stack, grad_out, grad_u_below, near, sums, total_out, blocks = rest
    scenes, rows, cols, ch = grad_u.shape
    put_blocks(weights.at[section], blocks)
    terms, total = back_terms(section, count, pieces, grads, gbs)
    total_out[...] = total
    mean_below, inv_below, _ = norm_stats(summed(pieces_below), count_below)
    make_rows = back_rows(count, last, terms, stack, grad_u, g1, pre, p1, slope)
    outer_row = back_outer_row(section, count, last, terms, g2, p2, pieces, gbs, cols)

    def make_all(scene):
        make_rows(scene)
        put_row(stack, scene, rows + 1, outer_row(scene), True)

    first = second = None
    make_all(0)
    for scene in range(scenes):
        if scene + 1 < scenes:
            make_all(scene + 1)
        for p in range(rows // 2):
            both = conv_back_pair(stack, None, blocks, scene, p)
            for m in range(2):
                r = 2 * p + m
                grad = grad_row(grad_in, last, scene, r, rows).astype(f32)
                grad = (grad + both[:, m * ch : (m + 1) * ch]).astype(bf16)
                grad_out[scene, r] = grad
                if r == 0:
                    near[scene * cols : (scene + 1) * cols, :] = grad
                lifted = grad.astype(f32) * slope_below[scene, r + 1]
                grad_u_below[scene, r] = lifted
                first = plus(first, fold(lifted * pre_below[scene, r]))
                second = plus(second, fold(lifted))
    put_sums(sums, near, grad_sums(first, second, mean_below, inv_below))


def final_weight_kernel(section, count, last, n, *rest):
    pieces, rest = rest[:n], rest[n:]
    grads, rest = rest[:n], rest[n:]
    grad_u, g1, pre, p1, slope, gbs, x, stack, mine, theirs, total_out, whole = rest
    terms, total = back_terms(section, count, pieces, grads, gbs)
    total_out[...] = total
    make_rows = back_rows(count, last, terms, stack, grad_u, g1, pre, p1, slope)
    weight_body(x, stack, mine, theirs, whole, make_rows)


def final_grad_kernel(section, count, last, n, *rest):
    pieces, rest = rest[:n], rest[n:]
    grads, rest = rest[:n], rest[n:]
    grad_in, g2, pre, p2, gbs, weights, stack, grad_out, outer, blocks = rest
    scenes, rows, cols, ch = grad_out.shape[1:]
    put_blocks(weights.at[section], blocks)
    terms, _ = back_terms(section, count, pieces, grads, gbs)
    outer_row = back_outer_row(section, count, last, terms, g2, p2, pieces, gbs, cols)
    place = Place()

    @pl.loop(0, scenes)
    def _(scene):
        put_outer(outer, scene, outer_row(scene), True)
        for p in range(rows // 2):
            both = conv_back_pair(stack, outer, blocks, scene, p)
            for m in range(2):
                r = 2 * p + m
                grad = grad_row(grad_in, last, scene, r, rows).astype(f32)
                grad = grad + both[:, m * ch : (m + 1) * ch]
                if count is None:
                    grad = jnp.where(pre[scene, r] > hole_edge, grad, 0.0)
                grad_out[0, scene, place.row(r, rows)] = grad.astype(bf16)


def weight_kernel(x, stack, mine, theirs, whole):
    weight_body(x, stack, mine, theirs, whole, None)


def weight_body(x, stack, mine, theirs, whole, make_rows):
    scenes, padded, cols, ch = x.shape
    rows = padded - 2
    place = Place()
    total = None
    if make_rows:
        make_rows(0)
    for scene in range(scenes):
        if make_rows and scene + 1 < scenes:
            make_rows(scene + 1)
        lines = [x[scene, k] for k in range(rows + 2)]
        lhs = jnp.concatenate(
            [jnp.concatenate(lines[i : i + rows], axis=0) for i in range(3)], axis=1
        )
        rhs = jnp.concatenate(
            [
                jnp.concatenate(
                    [
                        stack[j, k // 2, scene, :, (k % 2) * ch : (k % 2 + 1) * ch]
                        for j in range(3)
                    ],
                    axis=1,
                )
                for k in range(1, rows + 1)
            ],
            axis=0,
        )
        term = lax.dot_general(lhs, rhs, (((0,), (0,)), ((), ())), preferred_element_type=f32)
        total = plus(total, term)
    for i in range(3):
        for j in range(3):
            at = pl.multiple_of((3 * place.tap(i) + j) * ch, 8)
            whole[pl.ds(at, ch), :] = total[i * ch : (i + 1) * ch, j * ch : (j + 1) * ch]
    chips, chunk = mine.shape[:2]
    for z in range(chips):
        at = pl.multiple_of((2 * z + place.core) * chunk, 8)
        mine[z] = whole[pl.ds(at, chunk), :]
        at = pl.multiple_of((2 * z + 1 - place.core) * chunk, 8)
        theirs[z] = whole[pl.ds(at, chunk), :].astype(bf16)


def chip_kernel(n, *refs):
    mine, refs = refs[:n], refs[n:]
    theirs, refs = refs[:n], refs[n:]
    totals, refs = refs[:n], refs[n:]
    outs, held, sums = refs[:4], refs[4], refs[5]
    here = Place().section
    chips, chunk, ch = mine[0].shape
    for s in range(n):
        for z in range(chips):
            held[s, z * chunk : (z + 1) * chunk] = mine[s][z] + theirs[s][z].astype(f32)
        sums[s] = totals[s][...]
    size = chips * chunk
    for d in range(4):
        if d:
            outs[d][:size] = held[here ^ d].astype(bf16)
            put_parts(outs[d], size, sums[here ^ d])
        else:
            outs[0][:size] = held[here]
            outs[0][size:] = sums[here]


def section_kernel(own, a, b, c, mine, one, two, three, sums, held):
    chips, chunk = held.shape[:2]
    size = chips * chunk
    for z in range(chips):
        at = slice(z * chunk, (z + 1) * chunk)
        held[z] = own[at] + a[at].astype(f32) + b[at].astype(f32) + c[at].astype(f32)
    total = own[size:]
    for got in (a, b, c):
        parts = got[size:].astype(f32)
        total = total + (parts[0:8] + parts[8:16] + parts[16:24])
    sums[...] = total
    chip = Place().chip
    mine[...] = held[chip]
    for k, out in ((1, one), (2, two), (3, three)):
        out[...] = held[chip ^ k].astype(bf16)


def last_kernel(mine, a, b, c, sums, weight, gain, bias):
    gain[...] = sums[0:1]
    bias[...] = sums[1:2]
    weight[0] = mine[...] + a[...].astype(f32) + b[...].astype(f32) + c[...].astype(f32)


def call(body, outs, ins, scratch=(), flops=0, name=None, hbm=()):
    specs = [VMEM_SPEC] * len(ins)
    for n in hbm:
        specs[n] = pl.BlockSpec(memory_space=pltpu.HBM)
    return pl.pallas_call(
        body,
        out_shape=[jax.ShapeDtypeStruct(s, d) for s, d in outs],
        in_specs=specs,
        out_specs=[VMEM_SPEC] * len(outs),
        scratch_shapes=list(scratch),
        compiler_params=pltpu.CompilerParams(vmem_limit_bytes=12 * 2**20),
        cost_estimate=pl.CostEstimate(flops=flops, bytes_accessed=0, transcendentals=0),
        name=name,
    )(*ins)


def swap(value, axis, step):
    count = lax.axis_size(axis)
    return lax.ppermute(value, axis, [(i, i ^ step) for i in range(count)])


def swap_next(value):
    pairs = []
    for i in range(1, lax.axis_size("row") - 1, 2):
        pairs += [(i, i + 1), (i + 1, i)]
    return lax.ppermute(value, "row", pairs)


def row_pieces(total):
    count = lax.axis_size("row")
    stride = 2
    while True:
        group = min(4, count // stride)
        pieces = [total] + [swap(total, "row", k * stride + (stride == 2)) for k in range(1, group)]
        stride *= group
        if stride >= count:
            return pieces
        total = sum(pieces[1:], pieces[0])


def after(value, signal):
    return lax.optimization_barrier((value, signal))[0]


def far_rows(rows_ref, *more):
    scenes, _, cols, ch = rows_ref.shape
    size = scenes * cols * (1 + len(more))
    (far,) = call(far_kernel, [((size, ch), bf16)], (rows_ref, *more), name="far")
    return far


def exchange(sums, near, rows_ref=None):
    got = swap(near, "row", 1)
    far = None if rows_ref is None else swap_next(far_rows(rows_ref))
    parts = got[got.shape[0] - 32 :].astype(f32)
    total = sums + (parts[0:8] + parts[8:16] + parts[16:24])
    return got, far, row_pieces(total), total


def per_device(features, conv_weight, norm_gain, norm_bias, valid_mask, out_cotangent):
    sections = lax.axis_size("section")
    tiles = lax.axis_size("row")
    scenes, rows, cols, ch = features.shape[1:]
    taps = conv_weight.shape[1]
    cells = float(scenes * rows * cols * tiles)
    tile_shape = (scenes, rows, cols, ch)
    pad_shape = (scenes, rows + 2, cols, ch)
    slope_shape = (scenes, rows + 1, cols, ch)
    edge = scenes * cols
    near_shape = (edge + 32, ch)
    sum_shape = (8, ch)
    stack_shape = (3, rows // 2 + 1, scenes, cols, 2 * ch)
    blocks = pltpu.VMEM((6, 2 * ch, 2 * ch), bf16)
    outer = pltpu.VMEM((3, scenes, cols, ch), bf16)
    flops = 2 * scenes * rows * cols * taps * ch
    half = taps // 2
    chunk = taps // tiles
    direct = tiles == 8 and chunk % 16 == 0

    def in_hbm(*values):
        return [pltpu.with_memory_space_constraint(v, pltpu.HBM) for v in values]

    e1, e2, cot_far, wsend = call(
        prep_kernel,
        [((2 * edge, ch), bf16), ((edge, ch), bf16), ((edge, ch), bf16), ((half + 32, ch), bf16)],
        in_hbm(valid_mask, features, out_cotangent, conv_weight, norm_gain, norm_bias),
        [
            pltpu.VMEM((4, scenes, cols, ch), bf16),
            pltpu.VMEM((1, scenes, rows, cols), jnp.int32),
            pltpu.VMEM((8, ch), f32),
            pltpu.SemaphoreType.DMA((8,)),
        ],
        hbm=range(6),
        name="prep",
    )
    got = [swap(wsend, "section", d) for d in (1, 2, 3)]
    e1 = swap(e1, "row", 1)
    e2 = swap_next(e2)
    others = [swap(v, "row", 1) for v in got]
    weights, gbs = call(
        gather_kernel,
        [((sections, taps, ch), bf16), ((sections, 8, ch), f32)],
        (conv_weight, norm_gain, norm_bias, *got, *others),
        name="gather",
    )

    forward_outs = [(pad_shape, bf16), (tile_shape, f32), (near_shape, bf16), (sum_shape, f32)]
    scratch = [pltpu.VMEM(stack_shape, bf16), blocks]
    kept = []
    slopes = []
    x, pre, near, sums = call(
        first_kernel,
        forward_outs,
        (valid_mask, features, e1, e2, weights),
        scratch,
        flops=flops,
        name="forward",
    )
    for section in range(sections):
        count = None if section == 0 else cells
        last = section == sections - 1
        near, far, pieces, total = exchange(sums, near, None if last else pre)
        if last:
            far = swap_next(far_rows(after(pre, total), cot_far))
        if section > 0:
            _, below, below_near, _, below_pieces, below_count = kept[-1]
            slopes += call(
                functools.partial(slope_kernel, section - 1, below_count, len(pieces)),
                [(slope_shape, f32)],
                (after(below, total), below_near, *below_pieces, gbs),
                flops=8 * flops if last else 0,
                name="slope",
            )
            pieces[0] = after(pieces[0], slopes[-1])
        kept.append((x, pre, near, far, pieces, count))
        if section == sections - 1:
            break
        x, pre, near, sums = call(
            functools.partial(next_kernel, section + 1, count, len(pieces)),
            forward_outs,
            (x, pre, near, far, *pieces, gbs, weights),
            scratch,
            flops=flops,
            name="forward",
        )
    n = len(pieces)
    grad_u, sums = call(
        functools.partial(turn_kernel, count, n, sections - 1),
        [(tile_shape, f32), (sum_shape, f32)],
        (pre, out_cotangent, *pieces, gbs),
        name="turn",
    )
    total = sums + swap(sums, "row", 1)
    grads = row_pieces(total)
    slopes += call(
        functools.partial(slope_kernel, sections - 1, count, n),
        [(slope_shape, f32)],
        (after(pre, total), near, *pieces, gbs),
        name="slope",
    )
    grad, g1, g2 = out_cotangent, e1, far
    parts = [None] * sections
    totals = [None] * sections
    part_shapes = [((tiles // 2, chunk, ch), f32), ((tiles // 2, chunk, ch), bf16)]
    whole = pltpu.VMEM((taps, ch), f32)
    for section in range(sections - 1, 0, -1):
        x, pre, p1, p2, pieces, count = kept[section]
        _, below, _, _, below_pieces, below_count = kept[section - 1]
        last = section == sections - 1
        stack, grad, grad_u, near, sums, totals[section] = call(
            functools.partial(back_kernel, section, count, below_count, last, n),
            [
                (stack_shape, bf16),
                (tile_shape, bf16),
                (tile_shape, f32),
                (near_shape, bf16),
                (sum_shape, f32),
                (sum_shape, f32),
            ],
            (
                *pieces,
                *grads,
                *below_pieces,
                below,
                slopes[section - 1],
                grad_u,
                grad,
                g1,
                g2,
                pre,
                p1,
                p2,
                slopes[section],
                gbs,
                weights,
            ),
            [blocks],
            flops=flops,
            name="backward",
        )
        g1, g2, grads, total = exchange(sums, near, grad if section > 1 else None)
        parts[section] = call(
            weight_kernel,
            part_shapes,
            (x, after(stack, total)),
            [whole],
            flops=flops,
            name="weight",
        )
        grads[0] = after(grads[0], parts[section][1])
    x, pre, p1, p2, pieces, count = kept[0]
    last = sections == 1
    stack, *parts[0], totals[0] = call(
        functools.partial(final_weight_kernel, 0, count, last, n),
        [(stack_shape, bf16), *part_shapes, (sum_shape, f32)],
        (*pieces, *grads, grad_u, g1, pre, p1, slopes[0], gbs, x),
        [whole],
        flops=flops,
        name="weight",
    )

    def finish_neck(signal):
        far = swap_next(far_rows(after(grad, signal)))
        last_x, last_pre, _, _, last_pieces, last_count = kept[-1]
        (neck,) = call(
            functools.partial(neck_kernel, last_count, n, sections - 1),
            [((1,) + tile_shape, bf16)],
            (last_x, after(last_pre, signal), *last_pieces, gbs),
            flops=8 * flops,
            name="neck",
        )
        return neck, far

    def finish_grad(far, signal):
        (feature_grad,) = call(
            functools.partial(final_grad_kernel, 0, count, last, n),
            [((1,) + tile_shape, bf16)],
            (*pieces, *grads, grad, far, pre, p2, gbs, weights, after(stack, signal)),
            [outer, blocks],
            flops=flops,
            name="final_grad",
        )
        return feature_grad

    m = sections
    if direct:
        size = taps // 2
        theirs = [swap(p[1], "row", 1) for p in parts]
        own, *sending = call(
            functools.partial(chip_kernel, m),
            [((size + 8, ch), f32)] + [((size + 32, ch), bf16)] * 3,
            (*[p[0] for p in parts], *theirs, *totals),
            [pltpu.VMEM((m, size, ch), f32), pltpu.VMEM((m, 8, ch), f32)],
            name="chips",
        )
        received = [swap(v, "section", d + 1) for d, v in enumerate(sending)]
        neck, far = finish_neck(own)
        received[0] = after(received[0], neck)
        mine, one, two, three, total = call(
            section_kernel,
            [((chunk, ch), f32)] + [((chunk, ch), bf16)] * 3 + [(sum_shape, f32)],
            (own, *received),
            [pltpu.VMEM((tiles // 2, chunk, ch), f32)],
            name="sections",
        )
        chunks = [swap(v, "row", 2 * (k + 1)) for k, v in enumerate((one, two, three))]
        feature_grad = finish_grad(far, total)
        mine = after(mine, feature_grad)
        weight_grad, gain_grad, bias_grad = call(
            last_kernel,
            [((1, chunk, ch), f32), ((1, ch), f32), ((1, ch), f32)],
            (mine, *chunks, total),
            name="last",
        )
    else:
        lanes = [list(range(c, tiles, 2)) for c in range(2)]
        here = lax.axis_index("section")
        chip_sums = jnp.stack([p[0] + swap(p[1], "row", 1).astype(f32) for p in parts])
        sums = jnp.stack(totals)

        def over_sections(stacked):
            total, *others = [
                lax.dynamic_index_in_dim(stacked, here ^ d, 0, keepdims=False) for d in range(4)
            ]
            for d, other in enumerate(others):
                total = total + swap(other, "section", d + 1)
            return total

        chip_sum, total = over_sections(chip_sums), over_sections(sums)
        weight_grad = lax.psum_scatter(
            chip_sum, "row", scatter_dimension=0, tiled=True, axis_index_groups=lanes
        )
        gain_grad, bias_grad = total[0:1], total[1:2]
        neck, far = finish_neck(total)
        feature_grad = finish_grad(far, neck)
    return neck, feature_grad, weight_grad, gain_grad, bias_grad


def solution(mesh):
    return jax.shard_map(
        per_device,
        mesh=mesh,
        in_specs=(
            P("section", None, "row", None, None),
            P("section", None, None),
            P("section", None),
            P("section", None),
            P(None, None, "row", None),
            P("section", None, "row", None, None),
        ),
        out_specs=(
            P("section", None, "row", None, None),
            P("section", None, "row", None, None),
            P("section", "row", None),
            P("section", None),
            P("section", None),
        ),
        check_vma=False,
    )
```
